32 devices in a mesh: ctx: 16 (over z, y, x), tp: 2 (over core).
Axes of the slice: x: 2, y: 2, z: 4, core: 2. Of those that a mesh axis runs over, the one named last changes fastest.
Arguments:
- queries: bfloat16 [2048, 64, 128], P(('ctx', 'tp')), may hold values from -24 to 24
- rotated_key_rows: bfloat16 [2048, 8, 128], P(('ctx', 'tp')), may hold values from -24 to 24
- unscaled_value_rows: bfloat16 [2048, 8, 128], P(('ctx', 'tp')), may hold values from -6 to 6
- key_block_scales: bfloat16 [16, 8], P('ctx', 'tp'), may hold values from 0.5 to 2
- value_block_scales: bfloat16 [16, 8], P('ctx', 'tp'), may hold values from 0.5 to 2
- doc_lengths: int32 [16], replicated, may hold values from 1 to 512, 2048 in all
Outputs:
- attended: bfloat16 [2048, 64, 128], P(('ctx', 'tp'))
The draws below stay inside these ranges and needn't reach their ends.
Inputs may be any that keep to these rules, and one draw needn't show every extreme that they name: `doc_lengths`: they sum to 2048; the longest is exactly 512.
All inputs are finite; a program needn't handle non-finite values.
Results may differ from the reference program's by a relative error of at most 0.0035.
Values may be sent and summed in bfloat16 or wider, within the bound.
No kernel may reach another device: no remote copies, remote signals or barrier semaphores. Data moves between devices by JAX's collectives and lax.ppermute only.
A program may use at most 64 MiB of HBM per device.

```python
import math
import jax
import jax.numpy as jnp
import numpy as np
from jax import lax

QUERY_HEADS = 64
KEY_VALUE_HEADS = 8
HEAD_WIDTH = 128
SCALE_BLOCK = 128
TOKENS_PER_SHARD = 128
DOCUMENT_LIMIT = 512
PACKED_TOKENS = 2048
NDOCS = 16


def draw_queries(key, part):
    own_part = jnp.clip(jax.random.normal(jax.random.fold_in(key, 11), (PACKED_TOKENS, QUERY_HEADS, HEAD_WIDTH), jnp.float32), -4.0, 4.0)
    return own_part.astype(jnp.bfloat16)


def draw_rotated_key_rows(key, part):
    own_part = jnp.clip(jax.random.normal(jax.random.fold_in(key, 12), (PACKED_TOKENS, KEY_VALUE_HEADS, HEAD_WIDTH), jnp.float32), -4.0, 4.0)
    return own_part.astype(jnp.bfloat16)


def steps_of(stream_key, dims, cuts, smallest, high):
    def one(position, shards_of):
        heights = jax.random.uniform(jax.random.fold_in(jax.random.fold_in(stream_key, 6), position), (shards_of,), jnp.float32, smallest / len(cuts), high / len(cuts))
        return jnp.repeat(jnp.exp(heights), dims[position] // shards_of).reshape((-1,) + (1,) * (len(dims) - position - 1))

    factor_of = one(*cuts[0])
    for cut in cuts[1:]:
        factor_of = factor_of * one(*cut)
    return factor_of


def profile(count, total, limit, lean):
    portions = [(1 << 20) // math.isqrt(grade ** lean) + 1 for grade in range(2, count + 1)]
    surplus, counts = total - limit - (count - 1), [1] * (count - 1)
    while surplus > 0:
        candidates = [i for i in range(count - 1) if counts[i] < limit]
        whole, left = sum([portions[i] for i in candidates]), surplus
        for i in candidates:
            more = min(limit - counts[i], max(1, left * portions[i] // whole), surplus)
            counts[i] = counts[i] + more
            surplus = surplus - more
    return np.array([limit] + counts)


def uneven(own_key, count, total, bound, lean):
    if count == 2:
        one = jax.random.randint(own_key, (), max(1, total - bound), min(bound, total - 1) + 1)
        return jnp.stack([one, total - one])
    sizes = jnp.asarray(profile(count, total, bound, lean), jnp.int32)
    twos = (count - 1) // 2
    giver, receiver = sizes[1:1 + 2 * twos:2], sizes[2:2 + 2 * twos:2]
    slack = jnp.minimum(giver - 1, bound - receiver)
    passed = jax.random.randint(jax.random.fold_in(own_key, 1), (twos,), 0, 1 << 20) % (slack + 1)
    sizes = sizes.at[1:1 + 2 * twos:2].set(giver - passed).at[2:2 + 2 * twos:2].set(receiver + passed)
    return sizes[jax.random.permutation(jax.random.fold_in(own_key, 2), count)]


def noise(key, shape, deviation, limit, cuts=(), held_as=jnp.bfloat16):
    result = deviation * jax.random.normal(key, shape, jnp.float32)
    if cuts:
        result = result * steps_of(key, shape, cuts, -0.22, 0.18)
    return jnp.clip(result, -limit, limit).astype(held_as)


def setup_inputs(seed: int = 0) -> dict:
    seeds = jax.random.split(jax.random.key(seed), 7)
    return {
        "queries": draw_queries(jax.random.fold_in(seeds[6], 71), 0),
        "rotated_key_rows": draw_rotated_key_rows(jax.random.fold_in(seeds[6], 71), 0),
        "unscaled_value_rows": noise(seeds[2], (PACKED_TOKENS, KEY_VALUE_HEADS, HEAD_WIDTH), 1.0, 6.0, ((0, 32),)),
        "key_block_scales": jnp.clip(jnp.exp(math.log(2.0) - 1.3862944 * jax.random.uniform(seeds[3], (PACKED_TOKENS // SCALE_BLOCK, KEY_VALUE_HEADS), jnp.float32) ** steps_of(seeds[3], (PACKED_TOKENS // SCALE_BLOCK, KEY_VALUE_HEADS), ((0, 16), (1, 2)), -0.2, 0.2)), 0.5, 2.0).astype(jnp.bfloat16),
        "value_block_scales": jnp.clip(jnp.exp(math.log(2.0) - 1.3862944 * jax.random.uniform(seeds[4], (PACKED_TOKENS // SCALE_BLOCK, KEY_VALUE_HEADS), jnp.float32) ** steps_of(seeds[4], (PACKED_TOKENS // SCALE_BLOCK, KEY_VALUE_HEADS), ((0, 16), (1, 2)), -0.2, 0.2)), 0.5, 2.0).astype(jnp.bfloat16),
        "doc_lengths": uneven(seeds[5], NDOCS, PACKED_TOKENS, DOCUMENT_LIMIT, 2).astype(jnp.int32),
    }


def document_of(positions, ends):
    return lax.optimization_barrier(jnp.sum((positions[:, None] >= ends[None, :]).astype(jnp.int32), axis=1)).astype(jnp.int32)

def reference(queries, rotated_key_rows, unscaled_value_rows, key_block_scales, value_block_scales, doc_lengths):
    query_group = QUERY_HEADS // KEY_VALUE_HEADS
    token_span = DOCUMENT_LIMIT + TOKENS_PER_SHARD
    ends = jnp.cumsum(doc_lengths).astype(jnp.int32)
    key_padding = jnp.concatenate([jnp.zeros((DOCUMENT_LIMIT, KEY_VALUE_HEADS, HEAD_WIDTH), rotated_key_rows.dtype), rotated_key_rows], axis=0)
    value_padding = jnp.concatenate([jnp.zeros((DOCUMENT_LIMIT, KEY_VALUE_HEADS, HEAD_WIDTH), unscaled_value_rows.dtype), unscaled_value_rows], axis=0)
    key_scale = jnp.repeat(key_block_scales, SCALE_BLOCK, axis=0)
    value_scale = jnp.repeat(value_block_scales, SCALE_BLOCK, axis=0)
    key_scale_padding = jnp.concatenate([jnp.ones((DOCUMENT_LIMIT, KEY_VALUE_HEADS), key_scale.dtype), key_scale], axis=0)
    value_scale_padding = jnp.concatenate([jnp.ones((DOCUMENT_LIMIT, KEY_VALUE_HEADS), value_scale.dtype), value_scale], axis=0)
    pad_pos = jnp.arange(PACKED_TOKENS + DOCUMENT_LIMIT, dtype=jnp.int32) - DOCUMENT_LIMIT
    pad_doc = document_of(pad_pos, ends)

    def one_block(index):
        start_offset = (index * TOKENS_PER_SHARD).astype(jnp.int32)
        query_rows = lax.dynamic_slice_in_dim(queries, start_offset, TOKENS_PER_SHARD, 0).astype(jnp.float32)
        query_rows = query_rows.reshape(TOKENS_PER_SHARD, KEY_VALUE_HEADS, query_group, HEAD_WIDTH)
        key_vectors = lax.dynamic_slice_in_dim(key_padding, start_offset, token_span, 0).astype(jnp.float32)
        value_vectors = lax.dynamic_slice_in_dim(value_padding, start_offset, token_span, 0).astype(jnp.float32)
        key_scale_local = lax.dynamic_slice_in_dim(key_scale_padding, start_offset, token_span, 0).astype(jnp.float32)
        vscl = lax.dynamic_slice_in_dim(value_scale_padding, start_offset, token_span, 0).astype(jnp.float32)
        q_pos = start_offset + jnp.arange(TOKENS_PER_SHARD, dtype=jnp.int32)
        q_doc = document_of(q_pos, ends)
        k_pos = lax.dynamic_slice_in_dim(pad_pos, start_offset, token_span, 0)
        k_doc = lax.dynamic_slice_in_dim(pad_doc, start_offset, token_span, 0)
        allowed = (k_doc[None, :] == q_doc[:, None]) & (k_pos[None, :] <= q_pos[:, None]) & (k_pos[None, :] >= 0)
        mask_four = allowed[:, None, None, :]
        scores = jnp.einsum('qkgd,jkd->qkgj', query_rows, key_vectors) / math.sqrt(HEAD_WIDTH) * key_scale_local.T[None, :, None, :]
        scores = jnp.where(mask_four, scores, -1e+30)
        top = lax.optimization_barrier(jnp.max(scores, axis=3, keepdims=True))
        expo = jnp.where(mask_four, jnp.exp(scores - top), 0.0)
        total = lax.optimization_barrier(jnp.sum(expo, axis=3))
        weights = (expo * vscl.T[None, :, None, :]).astype(jnp.bfloat16)
        weights = lax.optimization_barrier(weights).astype(jnp.float32)
        summed = jnp.einsum('qkgj,jkd->qkgd', weights, value_vectors)
        return (summed / total[..., None]).reshape(TOKENS_PER_SHARD, QUERY_HEADS, HEAD_WIDTH).astype(jnp.bfloat16)
    blocks = lax.map(one_block, jnp.arange(PACKED_TOKENS // TOKENS_PER_SHARD, dtype=jnp.int32))
    return blocks.reshape(PACKED_TOKENS, QUERY_HEADS, HEAD_WIDTH)
```

```python
import functools
import math

import jax
import jax.numpy as jnp
from jax import lax
from jax.experimental import pallas as pl
from jax.experimental.pallas import tpu as pltpu
from jax.sharding import PartitionSpec as P

NEG = -1e30
VMEM = pltpu.MemorySpace.VMEM
SMEM = pltpu.MemorySpace.SMEM


def pack_kernel(k_ref, v_ref, s_ref, out_ref, rows_ref):
    tokens, heads, width = k_ref.shape
    for part, ref in enumerate((k_ref, v_ref)):
        rows_ref[part] = ref[...].astype(jnp.float32).reshape(tokens * heads, width)
        for head in range(heads):
            start = (part * heads + head) * tokens
            out_ref[start : start + tokens, :] = rows_ref[part, pl.ds(head, tokens, stride=heads), :].astype(
                out_ref.dtype
            )
    out_ref[2 * heads * tokens :, :] = s_ref[...]


def pack(keys, values, scales):
    tokens, heads, width = keys.shape
    return pl.pallas_call(
        pack_kernel,
        out_shape=jax.ShapeDtypeStruct((2 * heads * tokens + scales.shape[0], width), keys.dtype),
        in_specs=[pl.BlockSpec(memory_space=VMEM)] * 3,
        out_specs=pl.BlockSpec(memory_space=VMEM),
        scratch_shapes=[pltpu.VMEM((2, tokens * heads, width), jnp.float32)],
        compiler_params=pltpu.CompilerParams(vmem_limit_bytes=8 * 2**20),
        name="pack",
    )(keys, values, scales)


def attend_kernel(count, heads, group, place_ref, length_ref, q_ref, *refs):
    mine, sibling = refs[:count], refs[count : 2 * count]
    out_ref, bias_ref = refs[2 * count :]
    tokens, step_heads, width = q_ref.shape
    rows = tokens * group
    block = 2 * tokens
    core = place_ref[1]
    step = pl.program_id(0)

    @pl.when(step == 0)
    def _():
        position = place_ref[0] + lax.broadcasted_iota(jnp.int32, (rows, width), 0) // group

        def later(i, carry):
            start, end = carry
            end = end + length_ref[i]
            return jnp.where(position >= end, end, start), end

        start, _ = lax.fori_loop(0, length_ref.shape[0], later, (jnp.zeros_like(position), jnp.int32(0)))
        lane = lax.broadcasted_iota(jnp.int32, (rows, width), 1)
        half = jnp.where(lane < tokens, core, 1 - core) * tokens + jnp.where(lane < tokens, lane, lane - tokens)
        for b in range(count):
            key = place_ref[2 + b] + half
            allowed = (key >= start) & (key <= position)
            bias_ref[:, b * block : (b + 1) * block] = jnp.where(allowed, 0.0, NEG)

    kv_local = heads // 2
    first = core == 0
    scale_rows = []
    for b in range(count):
        low = 2 * heads * tokens
        a = mine[b][low : low + 16, :].astype(jnp.float32)
        z = sibling[b][low : low + 16, :].astype(jnp.float32)
        scale_rows.append((jnp.where(first, a, z), jnp.where(first, z, a)))

    def pick(b, which, head):
        lower, upper = scale_rows[b]
        both = jnp.concatenate([lower[which * kv_local : which * kv_local + kv_local], upper[which * kv_local : which * kv_local + kv_local]], axis=0)
        row = lax.broadcasted_iota(jnp.int32, both.shape, 0)
        return jnp.sum(jnp.where(row == head, both, 0.0), axis=0, keepdims=True)

    for sub in range(step_heads // group):
        head = step * (step_heads // group) + sub
        q = q_ref[:, sub * group : (sub + 1) * group, :].reshape(rows, width)
        at_k = pl.multiple_of(head * tokens, tokens)
        at_v = pl.multiple_of((heads + head) * tokens, tokens)
        keys = jnp.concatenate(
            [ref[pl.ds(at_k, tokens), :] for b in range(count) for ref in (mine[b], sibling[b])], axis=0
        )
        values = jnp.concatenate(
            [ref[pl.ds(at_v, tokens), :] for b in range(count) for ref in (mine[b], sibling[b])], axis=0
        )
        k_scale = jnp.concatenate([pick(b, 0, head) for b in range(count)], axis=1)
        k_scale = k_scale * (math.log2(math.e) / math.sqrt(width))
        v_scale = jnp.concatenate([pick(b, 1, head) for b in range(count)], axis=1)
        scores = lax.dot_general(q, keys, (((1,), (1,)), ((), ())), preferred_element_type=jnp.float32)
        scores = scores * k_scale + bias_ref[...]
        top = jnp.max(scores, axis=1, keepdims=True)
        expo = jnp.exp2(scores - top)
        total = jnp.sum(expo, axis=1, keepdims=True)
        weights = (expo * v_scale).astype(jnp.bfloat16)
        summed = jnp.dot(weights, values, preferred_element_type=jnp.float32)
        out = (summed / total).astype(out_ref.dtype)
        out_ref[:, sub * group : (sub + 1) * group, :] = out.reshape(tokens, group, width)


def attend(queries, place, lengths, mine, sibling, heads):
    tokens, q_heads, width = queries.shape
    group = q_heads // heads
    count = len(mine)
    per_step = 2 * group
    whole = pl.BlockSpec(memory_space=VMEM)
    return pl.pallas_call(
        functools.partial(attend_kernel, count, heads, group),
        out_shape=jax.ShapeDtypeStruct(queries.shape, queries.dtype),
        grid=(q_heads // per_step,),
        in_specs=[
            pl.BlockSpec(memory_space=SMEM),
            pl.BlockSpec(memory_space=SMEM),
            pl.BlockSpec((tokens, per_step, width), lambda i: (0, i, 0)),
        ]
        + [whole] * (2 * count),
        out_specs=pl.BlockSpec((tokens, per_step, width), lambda i: (0, i, 0)),
        scratch_shapes=[pltpu.VMEM((tokens * group, count * 2 * tokens), jnp.float32)],
        compiler_params=pltpu.CompilerParams(vmem_limit_bytes=32 * 2**20),
        cost_estimate=pl.CostEstimate(
            flops=4 * tokens * q_heads * count * 2 * tokens * width,
            bytes_accessed=4 * tokens * q_heads * width,
            transcendentals=tokens * q_heads * count * 2 * tokens,
        ),
        name="attend",
    )(place, lengths, queries, *mine, *sibling)


def shards(queries, keys, values, key_scales, value_scales, lengths):
    tokens, heads, width = keys.shape
    ranks = lax.axis_size("ctx")
    c, t = lax.axis_index("ctx"), lax.axis_index("tp")
    block = tokens * lax.axis_size("tp")
    scales = jnp.concatenate([key_scales[0], value_scales[0]])
    scales = jnp.broadcast_to(scales[:, None], (scales.shape[0], width))
    scales = jnp.pad(scales, ((0, 16 - scales.shape[0]), (0, 0)))
    own = pack(keys, values, scales)

    def send(value, target):
        pairs = [(source, target(source)) for source in range(ranks)]
        return lax.ppermute(value, "ctx", [(i, j) for i, j in pairs if 0 <= j < ranks])

    def swap(value):
        return lax.ppermute(value, "tp", [(0, 1), (1, 0)])

    k = c % 4
    from_z = send(own, lambda i: i + 4)
    from_d = send(own, lambda i: i + (3 if i % 4 in (0, 2) else 1))
    to_x = jnp.where(k % 2 == 0, own, from_z)
    to_y = jnp.where(k < 2, own, from_z)
    from_x = send(to_x, lambda i: i ^ 1)
    from_y = send(to_y, lambda i: i ^ 2)
    mine = [own, from_z, from_d, from_x, from_y]
    back = [0, 4, jnp.where(k % 2 == 0, 1, 3), jnp.where(k % 2 == 0, 3, 1), 2]
    sibling = [swap(part) for part in mine]
    place = jnp.stack([c * block + t * tokens, t] + [(c - b) * block for b in back]).astype(jnp.int32)
    return attend(queries, place, lengths, mine, sibling, heads)


def solution(mesh):
    both = P(("ctx", "tp"), None, None)
    return jax.shard_map(
        shards,
        mesh=mesh,
        in_specs=(both, both, both, P("ctx", "tp"), P("ctx", "tp"), P()),
        out_specs=both,
        check_vma=False,
    )
```

```python
import functools
import math

import jax
import jax.numpy as jnp
from jax import lax
from jax.experimental import pallas as pl
from jax.experimental.pallas import tpu as pltpu
from jax.sharding import PartitionSpec as P

NEG = -1e30
VMEM = pltpu.MemorySpace.VMEM
SMEM = pltpu.MemorySpace.SMEM
HBM = pltpu.MemorySpace.HBM
F32 = jnp.float32
BF16 = jnp.bfloat16
WHOLE = pl.BlockSpec(memory_space=VMEM)
SCALE_ROWS = 16
CHUNK = 256


def pack_kernel(k_ref, v_ref, ks_ref, vs_ref, out_ref, rows_ref):
    tokens, heads, width = k_ref.shape
    for part, ref in enumerate((k_ref, v_ref)):
        rows_ref[part] = ref[...].astype(F32).reshape(tokens * heads, width)
        for head in range(heads):
            start = (part * heads + head) * tokens
            rows = rows_ref[part, pl.ds(head, tokens, stride=heads), :]
            out_ref[start : start + tokens, :] = rows.astype(out_ref.dtype)
    held = ks_ref.shape[1]
    row = lax.broadcasted_iota(jnp.int32, (SCALE_ROWS, held), 0)
    col = lax.broadcasted_iota(jnp.int32, (SCALE_ROWS, held), 1)
    k_scale = jnp.broadcast_to(ks_ref[...].astype(F32), row.shape)
    v_scale = jnp.broadcast_to(vs_ref[...].astype(F32), row.shape)
    both = jnp.where(row == col, k_scale, 0.0) + jnp.where(row == col + held, v_scale, 0.0)
    both = jnp.broadcast_to(jnp.sum(both, axis=1, keepdims=True), (SCALE_ROWS, width))
    out_ref[2 * heads * tokens :, :] = both.astype(out_ref.dtype)


def pack(keys, values, key_scales, value_scales):
    tokens, heads, width = keys.shape
    args = [pltpu.with_memory_space_constraint(x, HBM) for x in (keys, values, key_scales, value_scales)]
    return pl.pallas_call(
        pack_kernel,
        out_shape=jax.ShapeDtypeStruct((2 * heads * tokens + SCALE_ROWS, width), keys.dtype),
        grid=(1,),
        in_specs=[pl.BlockSpec(x.shape, lambda i, n=x.ndim: (0,) * n) for x in (keys, values, key_scales, value_scales)],
        out_specs=WHOLE,
        scratch_shapes=[pltpu.VMEM((2, tokens * heads, width), F32)],
        compiler_params=pltpu.CompilerParams(vmem_limit_bytes=8 * 2**20),
        name="pack",
    )(*args)


def scales_of(mine, sibling, heads, tokens, first):
    low = 2 * heads * tokens
    out = []
    for m, s in zip(mine, sibling):
        a, z = m[low:, :].astype(F32), s[low:, :].astype(F32)
        a, z = jnp.where(a > 0, a, 1.0), jnp.where(z > 0, z, 1.0)
        out.append((jnp.where(first, a, z), jnp.where(first, z, a)))
    return out


def attend_blocks(get_q, put, mask, mine, sibling, scale, heads, tokens, group, width, old):
    count = len(mine)
    block = 2 * tokens
    rows = tokens * group
    local = heads // 2
    chunk = min(CHUNK, rows)
    row_token = lax.broadcasted_iota(jnp.int32, (rows, width), 0) // group
    one_hot = jnp.where(row_token == lax.broadcasted_iota(jnp.int32, (rows, width), 1), 1.0, 0.0).astype(BF16)
    of_key = lax.broadcasted_iota(jnp.int32, (block * count, width), 0) // block
    ones = jnp.where(of_key == lax.broadcasted_iota(jnp.int32, (block * count, width), 1), 1.0, 0.0).astype(BF16)
    units = [(h, slice(r, r + chunk)) for h in range(heads) for r in range(0, rows, chunk)]
    ready = {}

    def stacked(at):
        return jnp.concatenate([r[at : at + tokens, :] for b in range(count) for r in (mine[b], sibling[b])], axis=0)

    def wide(x):
        return jnp.concatenate([x] * (chunk // width), axis=1)

    def prepared(h):
        if h not in ready:
            keys = jnp.concatenate([stacked(h * tokens), mask], axis=1)
            q = jnp.concatenate([get_q(h), one_hot], axis=1)
            part, at = h // local, h % local
            ks = [wide(s[part][at : at + 1, :] * (math.log2(math.e) / math.sqrt(width))) for s in scale]
            vs = [wide(s[part][local + at : local + at + 1, :]) for s in scale]
            ready[h] = keys, q, ks, [jnp.log2(v) for v in vs], [1.0 / v for v in vs]
        return ready[h]

    def scores_of(h, cs):
        keys, q = prepared(h)[:2]
        return lax.dot_general(keys, q[cs], (((1,), (1,)), ((), ())), preferred_element_type=F32)

    def softmax(h, cs, scores):
        ks, lv = prepared(h)[2:4]
        parts = [scores[b * block : (b + 1) * block] * ks[b] for b in range(count)]
        top = functools.reduce(jnp.maximum, [jnp.max(p, axis=0, keepdims=True) for p in parts])
        factor = None
        if old is not None:
            before = old[0][h : h + 1, cs]
            top = jnp.maximum(top, before)
            factor = jnp.exp2(before - top)
        weights = [jnp.exp2(parts[b] - (top - lv[b])).astype(BF16) for b in range(count)]
        return jnp.concatenate(weights, axis=0), top, factor

    def finish(h, cs, weights, top, factor):
        iv = prepared(h)[4]
        values = jnp.concatenate([stacked((heads + h) * tokens), ones], axis=1)
        acc = lax.dot_general(values, weights, (((0,), (0,)), ((), ())), preferred_element_type=F32)
        total = functools.reduce(jnp.add, [acc[width + b : width + b + 1] * iv[b] for b in range(count)])
        acc = acc[:width]
        if factor is not None:
            total = total + old[1][h : h + 1, cs] * factor
            acc = acc + old[2][h, :, cs] * factor
        put(h, cs, acc, top, total)

    scores = scores_of(*units[0])
    waiting = None
    for i, (h, cs) in enumerate(units):
        following = scores_of(*units[i + 1]) if i + 1 < len(units) else None
        done = softmax(h, cs, scores)
        if waiting is not None:
            finish(*waiting)
        waiting = (h, cs) + done
        scores = following
    finish(*waiting)


def early_kernel(count, late, heads, group, place_ref, length_ref, q_ref, *refs):
    mine, sibling = refs[:count], refs[count : 2 * count]
    acc_ref, top_ref, sum_ref, qh_ref, mask_ref, q_buf, q_sem = refs[2 * count :]
    tokens, _, width = q_ref.shape
    rows, block, pair = tokens * group, 2 * tokens, 2 * group
    copies = [
        pltpu.make_async_copy(q_ref.at[:, pl.ds(g * pair, pair), :], q_buf.at[g], q_sem.at[g]) for g in range(heads // 2)
    ]
    for copy in copies:
        copy.start()
    core = place_ref[1]
    position = place_ref[0] + lax.broadcasted_iota(jnp.int32, (8, width), 1)

    def later(i, carry):
        start, end = carry
        end = end + length_ref[i]
        return jnp.where(position >= end, end, start), end

    start, _ = lax.fori_loop(0, length_ref.shape[0], later, (jnp.zeros_like(position), jnp.int32(0)))
    start, position = start[:1], position[:1]
    i = lax.broadcasted_iota(jnp.int32, (block, width), 0)
    offset = jnp.where(i < tokens, core * tokens + i, (1 - core) * tokens + i - tokens)

    def mask(b):
        key = place_ref[2 + b] + offset
        return jnp.where((key >= start) & (key <= position), 0.0, NEG).astype(BF16)

    for b in range(late):
        mask_ref[b * block : (b + 1) * block, :] = mask(count + b)
    here = jnp.concatenate([mask(b) for b in range(count)], axis=0)
    scale = scales_of(mine, sibling, heads, tokens, core == 0)

    def get_q(h):
        if h % 2 == 0:
            copies[h // 2].wait()
        q = q_buf[h // 2][:, (h % 2) * group : (h % 2 + 1) * group, :].reshape(rows, width)
        qh_ref[h] = q
        return q

    def put(h, cs, acc, top, total):
        acc_ref[h, :, cs] = acc
        top_ref[h : h + 1, cs] = top
        sum_ref[h : h + 1, cs] = total

    attend_blocks(get_q, put, here, mine, sibling, scale, heads, tokens, group, width, None)


def last_kernel(count, heads, group, qh_ref, mask_ref, acc_ref, top_ref, sum_ref, *refs):
    mine, sibling = refs[:count], refs[count : 2 * count]
    out_ref, o_buf, o_sem = refs[2 * count :]
    _, rows, width = qh_ref.shape
    tokens, pair = rows // group, 2 * group
    scale = scales_of(mine, sibling, heads, tokens, lax.axis_index("tp") == 0)
    copies = []

    def put(h, cs, acc, top, total):
        out = (acc / total).T.astype(BF16)
        span = slice(cs.start // group, cs.stop // group)
        o_buf[h // 2, span, (h % 2) * group : (h % 2 + 1) * group, :] = out.reshape(span.stop - span.start, group, width)
        if h % 2 == 1 and cs.stop == rows:
            g = h // 2
            copies.append(pltpu.make_async_copy(o_buf.at[g], out_ref.at[:, pl.ds(g * pair, pair), :], o_sem.at[g]))
            copies[-1].start()

    attend_blocks(
        lambda h: qh_ref[h], put, mask_ref[...], mine, sibling, scale, heads, tokens, group, width, (top_ref, sum_ref, acc_ref)
    )
    for copy in copies:
        copy.wait()


def cost(tokens, q_heads, width, blocks):
    work = tokens * q_heads * blocks * 2 * tokens
    return pl.CostEstimate(flops=4 * work * width, bytes_accessed=2 * tokens * q_heads * width, transcendentals=work)


def early(queries, place, lengths, mine, sibling, late, heads):
    tokens, q_heads, width = queries.shape
    group, count = q_heads // heads, len(mine)
    rows = tokens * group
    shape = jax.ShapeDtypeStruct
    return pl.pallas_call(
        functools.partial(early_kernel, count, late, heads, group),
        out_shape=[
            shape((heads, width, rows), F32),
            shape((heads, rows), F32),
            shape((heads, rows), F32),
            shape((heads, rows, width), BF16),
            shape((late * 2 * tokens, width), BF16),
        ],
        in_specs=[pl.BlockSpec(memory_space=SMEM)] * 2 + [pl.BlockSpec(memory_space=HBM)] + [WHOLE] * (2 * count),
        out_specs=[WHOLE] * 5,
        scratch_shapes=[
            pltpu.VMEM((heads // 2, tokens, 2 * group, width), BF16),
            pltpu.SemaphoreType.DMA((heads // 2,)),
        ],
        compiler_params=pltpu.CompilerParams(vmem_limit_bytes=24 * 2**20),
        cost_estimate=cost(tokens, q_heads, width, count),
        name="early",
    )(place, lengths, pltpu.with_memory_space_constraint(queries, HBM), *mine, *sibling)


def last(state, mine, sibling, heads):
    acc, top, total, qh, mask = state
    _, rows, width = qh.shape
    count = len(mine)
    tokens = mask.shape[0] // (2 * count)
    group = rows // tokens
    return pl.pallas_call(
        functools.partial(last_kernel, count, heads, group),
        out_shape=jax.ShapeDtypeStruct((tokens, heads * group, width), BF16),
        in_specs=[WHOLE] * (5 + 2 * count),
        out_specs=pl.BlockSpec(memory_space=HBM),
        scratch_shapes=[
            pltpu.VMEM((heads // 2, tokens, 2 * group, width), BF16),
            pltpu.SemaphoreType.DMA((heads // 2,)),
        ],
        compiler_params=pltpu.CompilerParams(vmem_limit_bytes=24 * 2**20),
        cost_estimate=cost(tokens, heads * group, width, count),
        name="last",
    )(qh, mask, acc, top, total, *mine, *sibling)


def shards(queries, keys, values, key_scales, value_scales, lengths):
    tokens, heads, _ = keys.shape
    ranks = lax.axis_size("ctx")
    c, t = lax.axis_index("ctx"), lax.axis_index("tp")
    block = tokens * lax.axis_size("tp")
    own = pack(keys, values, key_scales, value_scales)

    def send(value, target):
        pairs = [(source, target(source)) for source in range(ranks)]
        return lax.ppermute(value, "ctx", [(i, j) for i, j in pairs if 0 <= j < ranks])

    def swap(value):
        return lax.ppermute(value, "tp", [(0, 1), (1, 0)])

    k = c % 4
    from_z = send(own, lambda i: (i + 4) % ranks)
    from_d = send(own, lambda i: i + (3 if i % 2 == 0 else 1))
    to_x = jnp.where(k % 2 == 0, own, from_z)
    to_y = jnp.where(k < 2, own, from_z)
    from_x = send(to_x, lambda i: i ^ 1)
    from_y = send(to_y, lambda i: i ^ 2)
    mine = [own, from_z, from_d, from_x, from_y]
    even = k % 2 == 0
    back = [0, 4, jnp.where(even, 1, 3), jnp.where(even, 3, 1), 2]
    sibling = [swap(part) for part in mine]
    place = jnp.stack([c * block + t * tokens, t] + [(c - b) * block for b in back]).astype(jnp.int32)
    state = early(queries, place, lengths, mine[:3], sibling[:3], 2, heads)
    return last(state, mine[3:], sibling[3:], heads)


def solution(mesh):
    both = P(("ctx", "tp"), None, None)
    return jax.shard_map(
        shards,
        mesh=mesh,
        in_specs=(both, both, both, P("ctx", "tp"), P("ctx", "tp"), P()),
        out_specs=both,
        check_vma=False,
    )
```

```python
import functools
import math

import jax
import jax.numpy as jnp
from jax import lax
from jax.experimental import pallas as pl
from jax.experimental.pallas import tpu as pltpu
from jax.sharding import PartitionSpec as P

NEG = -1e30
VMEM = pltpu.MemorySpace.VMEM
SMEM = pltpu.MemorySpace.SMEM
HBM = pltpu.MemorySpace.HBM
F32 = jnp.float32
BF16 = jnp.bfloat16
WHOLE = pl.BlockSpec(memory_space=VMEM)
SCALE_ROWS = 16
CHUNK = 256


def pack_kernel(k_ref, v_ref, ks_ref, vs_ref, out_ref, rows_ref):
    tokens, heads, width = k_ref.shape
    for part, ref in enumerate((k_ref, v_ref)):
        rows_ref[part] = ref[...].astype(F32).reshape(tokens * heads, width)
        for head in range(heads):
            start = (part * heads + head) * tokens
            rows = rows_ref[part, pl.ds(head, tokens, stride=heads), :]
            out_ref[start : start + tokens, :] = rows.astype(out_ref.dtype)
    held = ks_ref.shape[1]
    row = lax.broadcasted_iota(jnp.int32, (SCALE_ROWS, held), 0)
    col = lax.broadcasted_iota(jnp.int32, (SCALE_ROWS, held), 1)
    k_scale = jnp.broadcast_to(ks_ref[...].astype(F32), row.shape)
    v_scale = jnp.broadcast_to(vs_ref[...].astype(F32), row.shape)
    both = jnp.where(row == col, k_scale, 0.0) + jnp.where(row == col + held, v_scale, 0.0)
    both = jnp.broadcast_to(jnp.sum(both, axis=1, keepdims=True), (SCALE_ROWS, width))
    out_ref[2 * heads * tokens :, :] = both.astype(out_ref.dtype)


def pack(keys, values, key_scales, value_scales):
    tokens, heads, width = keys.shape
    args = [pltpu.with_memory_space_constraint(x, HBM) for x in (keys, values, key_scales, value_scales)]
    return pl.pallas_call(
        pack_kernel,
        out_shape=jax.ShapeDtypeStruct((2 * heads * tokens + SCALE_ROWS, width), keys.dtype),
        grid=(1,),
        in_specs=[pl.BlockSpec(x.shape, lambda i, n=x.ndim: (0,) * n) for x in (keys, values, key_scales, value_scales)],
        out_specs=WHOLE,
        scratch_shapes=[pltpu.VMEM((2, tokens * heads, width), F32)],
        compiler_params=pltpu.CompilerParams(vmem_limit_bytes=8 * 2**20),
        name="pack",
    )(*args)


def scales_of(mine, sibling, heads, tokens, first):
    low = 2 * heads * tokens
    out = []
    for m, s in zip(mine, sibling):
        a, z = m[low:, :].astype(F32), s[low:, :].astype(F32)
        a, z = jnp.where(a > 0, a, 1.0), jnp.where(z > 0, z, 1.0)
        out.append((jnp.where(first, a, z), jnp.where(first, z, a)))
    return out


def attend_blocks(get_q, put, mask, mine, sibling, scale, heads, tokens, group, width, old):
    count = len(mine)
    block = 2 * tokens
    rows = tokens * group
    local = heads // 2
    chunk = min(CHUNK, rows)
    row_token = lax.broadcasted_iota(jnp.int32, (rows, width), 0) // group
    one_hot = jnp.where(row_token == lax.broadcasted_iota(jnp.int32, (rows, width), 1), 1.0, 0.0).astype(BF16)
    of_key = lax.broadcasted_iota(jnp.int32, (block * count, width), 0) // block
    ones = jnp.where(of_key == lax.broadcasted_iota(jnp.int32, (block * count, width), 1), 1.0, 0.0).astype(BF16)
    units = [(h, slice(r, r + chunk)) for h in range(heads) for r in range(0, rows, chunk)]
    ready = {}

    def stacked(at):
        return jnp.concatenate([r[at : at + tokens, :] for b in range(count) for r in (mine[b], sibling[b])], axis=0)

    def wide(x):
        return jnp.concatenate([x] * (chunk // width), axis=1)

    def prepared(h):
        if h not in ready:
            keys = jnp.concatenate([stacked(h * tokens), mask], axis=1)
            q = jnp.concatenate([get_q(h), one_hot], axis=1)
            part, at = h // local, h % local
            ks = [wide(s[part][at : at + 1, :] * (math.log2(math.e) / math.sqrt(width))) for s in scale]
            vs = [wide(s[part][local + at : local + at + 1, :]) for s in scale]
            ready[h] = keys, q, ks, [jnp.log2(v) for v in vs], [1.0 / v for v in vs]
        return ready[h]

    def scores_of(h, cs):
        keys, q = prepared(h)[:2]
        return lax.dot_general(keys, q[cs], (((1,), (1,)), ((), ())), preferred_element_type=F32)

    def softmax(h, cs, scores):
        ks, lv = prepared(h)[2:4]
        parts = [scores[b * block : (b + 1) * block] * ks[b] for b in range(count)]
        top = functools.reduce(jnp.maximum, [jnp.max(p, axis=0, keepdims=True) for p in parts])
        factor = None
        if old is not None:
            before = old[0][h : h + 1, cs]
            top = jnp.maximum(top, before)
            factor = jnp.exp2(before - top)
        weights = [jnp.exp2(parts[b] - (top - lv[b])).astype(BF16) for b in range(count)]
        return jnp.concatenate(weights, axis=0), top, factor

    def finish(h, cs, weights, top, factor):
        iv = prepared(h)[4]
        values = jnp.concatenate([stacked((heads + h) * tokens), ones], axis=1)
        acc = lax.dot_general(values, weights, (((0,), (0,)), ((), ())), preferred_element_type=F32)
        total = functools.reduce(jnp.add, [acc[width + b : width + b + 1] * iv[b] for b in range(count)])
        acc = acc[:width]
        if factor is not None:
            total = total + old[1][h : h + 1, cs] * factor
            acc = acc + old[2][h, :, cs] * factor
        put(h, cs, acc, top, total)

    scores = scores_of(*units[0])
    waiting = None
    for i, (h, cs) in enumerate(units):
        following = scores_of(*units[i + 1]) if i + 1 < len(units) else None
        done = softmax(h, cs, scores)
        if waiting is not None:
            finish(*waiting)
        waiting = (h, cs) + done
        scores = following
    finish(*waiting)


def early_kernel(count, late, heads, group, place_ref, length_ref, q_ref, *refs):
    mine, sibling = refs[:count], refs[count : 2 * count]
    acc_ref, top_ref, sum_ref, qh_ref = refs[2 * count : 2 * count + 4]
    masks, (q_buf, q_sem) = refs[2 * count + 4 : -2], refs[-2:]
    tokens, _, width = q_ref.shape
    rows, block, pair = tokens * group, 2 * tokens, 2 * group
    copies = [
        pltpu.make_async_copy(q_ref.at[:, pl.ds(g * pair, pair), :], q_buf.at[g], q_sem.at[g]) for g in range(heads // 2)
    ]
    for copy in copies:
        copy.start()
    core = place_ref[1]
    position = place_ref[0] + lax.broadcasted_iota(jnp.int32, (8, width), 1)

    def later(i, carry):
        start, end = carry
        end = end + length_ref[i]
        return jnp.where(position >= end, end, start), end

    start, _ = lax.fori_loop(0, length_ref.shape[0], later, (jnp.zeros_like(position), jnp.int32(0)))
    start, position = start[:1], position[:1]
    i = lax.broadcasted_iota(jnp.int32, (block, width), 0)
    offset = jnp.where(i < tokens, core * tokens + i, (1 - core) * tokens + i - tokens)

    def mask(b):
        key = place_ref[2 + b] + offset
        return jnp.where((key >= start) & (key <= position), 0.0, NEG).astype(BF16)

    for b in range(late):
        masks[b][...] = mask(count + b)
    here = jnp.concatenate([mask(b) for b in range(count)], axis=0)
    scale = scales_of(mine, sibling, heads, tokens, core == 0)

    def get_q(h):
        if h % 2 == 0:
            copies[h // 2].wait()
        q = q_buf[h // 2][:, (h % 2) * group : (h % 2 + 1) * group, :].reshape(rows, width)
        qh_ref[h] = q
        return q

    def put(h, cs, acc, top, total):
        acc_ref[h, :, cs] = acc
        top_ref[h : h + 1, cs] = top
        sum_ref[h : h + 1, cs] = total

    attend_blocks(get_q, put, here, mine, sibling, scale, heads, tokens, group, width, None)


def middle_kernel(count, heads, group, qh_ref, mask_ref, acc_ref, top_ref, sum_ref, *refs):
    mine, sibling = refs[:count], refs[count : 2 * count]
    acc_out, top_out, sum_out = refs[2 * count :]
    _, rows, width = qh_ref.shape
    tokens = rows // group
    scale = scales_of(mine, sibling, heads, tokens, lax.axis_index("tp") == 0)

    def put(h, cs, acc, top, total):
        acc_out[h, :, cs] = acc
        top_out[h : h + 1, cs] = top
        sum_out[h : h + 1, cs] = total

    attend_blocks(
        lambda h: qh_ref[h], put, mask_ref[...], mine, sibling, scale, heads, tokens, group, width, (top_ref, sum_ref, acc_ref)
    )


def last_kernel(count, heads, group, qh_ref, acc_ref, top_ref, sum_ref, *refs):
    masks, mine, sibling = refs[:count], refs[count : 2 * count], refs[2 * count : 3 * count]
    out_ref, o_buf, o_sem = refs[3 * count :]
    _, rows, width = qh_ref.shape
    tokens, pair = rows // group, 2 * group
    scale = scales_of(mine, sibling, heads, tokens, lax.axis_index("tp") == 0)
    mask = jnp.concatenate([ref[...] for ref in masks], axis=0)
    copies = []

    def put(h, cs, acc, top, total):
        out = (acc / total).T.astype(BF16)
        span = slice(cs.start // group, cs.stop // group)
        o_buf[h // 2, span, (h % 2) * group : (h % 2 + 1) * group, :] = out.reshape(span.stop - span.start, group, width)
        if h % 2 == 1 and cs.stop == rows:
            g = h // 2
            copies.append(pltpu.make_async_copy(o_buf.at[g], out_ref.at[:, pl.ds(g * pair, pair), :], o_sem.at[g]))
            copies[-1].start()

    attend_blocks(
        lambda h: qh_ref[h], put, mask, mine, sibling, scale, heads, tokens, group, width, (top_ref, sum_ref, acc_ref)
    )
    for copy in copies:
        copy.wait()


def cost(tokens, q_heads, width, blocks):
    work = tokens * q_heads * blocks * 2 * tokens
    return pl.CostEstimate(flops=4 * work * width, bytes_accessed=2 * tokens * q_heads * width, transcendentals=work)


def early(queries, place, lengths, mine, sibling, late, heads):
    tokens, q_heads, width = queries.shape
    group, count = q_heads // heads, len(mine)
    rows = tokens * group
    shape = jax.ShapeDtypeStruct
    return pl.pallas_call(
        functools.partial(early_kernel, count, late, heads, group),
        out_shape=[
            shape((heads, width, rows), F32),
            shape((heads, rows), F32),
            shape((heads, rows), F32),
            shape((heads, rows, width), BF16),
        ]
        + [shape((2 * tokens, width), BF16)] * late,
        in_specs=[pl.BlockSpec(memory_space=SMEM)] * 2 + [pl.BlockSpec(memory_space=HBM)] + [WHOLE] * (2 * count),
        out_specs=[WHOLE] * (4 + late),
        scratch_shapes=[
            pltpu.VMEM((heads // 2, tokens, 2 * group, width), BF16),
            pltpu.SemaphoreType.DMA((heads // 2,)),
        ],
        compiler_params=pltpu.CompilerParams(vmem_limit_bytes=24 * 2**20),
        cost_estimate=cost(tokens, q_heads, width, count),
        name="early",
    )(place, lengths, pltpu.with_memory_space_constraint(queries, HBM), *mine, *sibling)


def middle(state, qh, mask, mine, sibling):
    heads, rows, width = qh.shape
    tokens = mask.shape[0] // 2
    group = rows // tokens
    return pl.pallas_call(
        functools.partial(middle_kernel, 1, heads, group),
        out_shape=[jax.ShapeDtypeStruct(x.shape, x.dtype) for x in state],
        in_specs=[WHOLE] * 7,
        out_specs=[WHOLE] * 3,
        compiler_params=pltpu.CompilerParams(vmem_limit_bytes=24 * 2**20),
        cost_estimate=cost(tokens, heads * group, width, 1),
        name="middle",
    )(qh, mask, *state, mine, sibling)


def last(state, qh, masks, mine, sibling):
    heads, rows, width = qh.shape
    count, tokens = len(mine), masks[0].shape[0] // 2
    group = rows // tokens
    return pl.pallas_call(
        functools.partial(last_kernel, count, heads, group),
        out_shape=jax.ShapeDtypeStruct((tokens, heads * group, width), BF16),
        in_specs=[WHOLE] * (4 + 3 * count),
        out_specs=pl.BlockSpec(memory_space=HBM),
        scratch_shapes=[
            pltpu.VMEM((heads // 2, tokens, 2 * group, width), BF16),
            pltpu.SemaphoreType.DMA((heads // 2,)),
        ],
        compiler_params=pltpu.CompilerParams(vmem_limit_bytes=24 * 2**20),
        cost_estimate=cost(tokens, heads * group, width, count),
        name="last",
    )(qh, *state, *masks, *mine, *sibling)


def shards(queries, keys, values, key_scales, value_scales, lengths):
    tokens, heads, _ = keys.shape
    ranks = lax.axis_size("ctx")
    c, t = lax.axis_index("ctx"), lax.axis_index("tp")
    block = tokens * lax.axis_size("tp")
    own = pack(keys, values, key_scales, value_scales)

    def send(value, target):
        pairs = [(source, target(source)) for source in range(ranks)]
        return lax.ppermute(value, "ctx", [(i, j) for i, j in pairs if 0 <= j < ranks])

    def swap(value):
        return lax.ppermute(value, "tp", [(0, 1), (1, 0)])

    k = c % 4
    from_z = send(own, lambda i: (i + 4) % ranks)
    from_d = send(own, lambda i: i + (3 if i % 2 == 0 else 1))
    to_x = jnp.where(k % 2 == 0, own, from_z)
    to_y = jnp.where(k < 2, own, from_z)
    from_x = send(to_x, lambda i: i ^ 1)
    from_y = send(to_y, lambda i: i ^ 2)
    even = k % 2 == 0
    back = [0, 4, jnp.where(even, 1, 3), jnp.where(even, 3, 1), 2]
    place = jnp.stack([c * block + t * tokens, t] + [(c - b) * block for b in back]).astype(jnp.int32)

    acc, top, total, qh, mask_d, mask_x, mask_y = early(
        queries, place, lengths, [own, from_z], [swap(own), swap(from_z)], 3, heads
    )
    from_d, top = lax.optimization_barrier((from_d, top))
    beside_d = swap(from_d)
    from_x, from_y, top, beside_d = lax.optimization_barrier((from_x, from_y, top, beside_d))
    beside = [swap(from_x), swap(from_y)]
    state = middle((acc, top, total), qh, mask_d, from_d, beside_d)
    return last(state, qh, [mask_x, mask_y], [from_x, from_y], beside)


def solution(mesh):
    both = P(("ctx", "tp"), None, None)
    return jax.shard_map(
        shards,
        mesh=mesh,
        in_specs=(both, both, both, P("ctx", "tp"), P("ctx", "tp"), P()),
        out_specs=both,
        check_vma=False,
    )
```

```python
import functools
import math

import jax
import jax.numpy as jnp
from jax import lax
from jax.experimental import pallas as pl
from jax.experimental.pallas import tpu as pltpu
from jax.sharding import PartitionSpec as P

NEG = -1e30
VMEM = pltpu.MemorySpace.VMEM
HBM = pltpu.MemorySpace.HBM
F32 = jnp.float32
BF16 = jnp.bfloat16
WHOLE = pl.BlockSpec(memory_space=VMEM)
SCALE_ROWS = 16
CHUNK = 256
GATHERED = 2


def pack_kernel(k_ref, v_ref, ks_ref, vs_ref, out_ref, rows_ref):
    tokens, heads, width = k_ref.shape
    for part, ref in enumerate((k_ref, v_ref)):
        rows_ref[part] = ref[...].astype(F32).reshape(tokens * heads, width)
        for head in range(heads):
            start = (part * heads + head) * tokens
            rows = rows_ref[part, pl.ds(head, tokens, stride=heads), :]
            out_ref[start : start + tokens, :] = rows.astype(out_ref.dtype)
    held = ks_ref.shape[1]
    row = lax.broadcasted_iota(jnp.int32, (SCALE_ROWS, held), 0)
    col = lax.broadcasted_iota(jnp.int32, (SCALE_ROWS, held), 1)
    k_scale = jnp.broadcast_to(ks_ref[...].astype(F32), row.shape)
    v_scale = jnp.broadcast_to(vs_ref[...].astype(F32), row.shape)
    both = jnp.where(row == col, k_scale, 0.0) + jnp.where(row == col + held, v_scale, 0.0)
    both = jnp.broadcast_to(jnp.sum(both, axis=1, keepdims=True), (SCALE_ROWS, width))
    out_ref[2 * heads * tokens :, :] = both.astype(out_ref.dtype)


def pack(keys, values, key_scales, value_scales):
    tokens, heads, width = keys.shape
    args = [pltpu.with_memory_space_constraint(x, HBM) for x in (keys, values, key_scales, value_scales)]
    return pl.pallas_call(
        pack_kernel,
        out_shape=jax.ShapeDtypeStruct((2 * heads * tokens + SCALE_ROWS, width), keys.dtype),
        grid=(1,),
        in_specs=[pl.BlockSpec(x.shape, lambda i, n=x.ndim: (0,) * n) for x in (keys, values, key_scales, value_scales)],
        out_specs=WHOLE,
        scratch_shapes=[pltpu.VMEM((2, tokens * heads, width), F32)],
        compiler_params=pltpu.CompilerParams(vmem_limit_bytes=8 * 2**20),
        name="pack",
    )(*args)


def scales_of(mine, sibling, heads, tokens, first):
    low = 2 * heads * tokens
    out = []
    for m, s in zip(mine, sibling):
        a, z = m[low:, :].astype(F32), s[low:, :].astype(F32)
        a, z = jnp.where(a > 0, a, 1.0), jnp.where(z > 0, z, 1.0)
        out.append((jnp.where(first, a, z), jnp.where(first, z, a)))
    return out


def attend_blocks(get_q, put, mask, mine, sibling, scale, heads, tokens, group, width, old):
    count = len(mine)
    block = 2 * tokens
    rows = tokens * group
    local = heads // 2
    chunk = min(CHUNK, rows)
    row_token = lax.broadcasted_iota(jnp.int32, (rows, width), 0) // group
    one_hot = jnp.where(row_token == lax.broadcasted_iota(jnp.int32, (rows, width), 1), 1.0, 0.0).astype(BF16)
    of_key = lax.broadcasted_iota(jnp.int32, (block * count, width), 0) // block
    ones = jnp.where(of_key == lax.broadcasted_iota(jnp.int32, (block * count, width), 1), 1.0, 0.0).astype(BF16)
    units = [(h, slice(r, r + chunk)) for h in range(heads) for r in range(0, rows, chunk)]
    ready = {}

    def stacked(at):
        return jnp.concatenate([r[at : at + tokens, :] for b in range(count) for r in (mine[b], sibling[b])], axis=0)

    def wide(x):
        return jnp.concatenate([x] * (chunk // width), axis=1)

    def prepared(h):
        if h not in ready:
            keys = jnp.concatenate([stacked(h * tokens), mask], axis=1)
            q = jnp.concatenate([get_q(h), one_hot], axis=1)
            part, at = h // local, h % local
            ks = [wide(s[part][at : at + 1, :] * (math.log2(math.e) / math.sqrt(width))) for s in scale]
            vs = [wide(s[part][local + at : local + at + 1, :]) for s in scale]
            ready[h] = keys, q, ks, [jnp.log2(v) for v in vs], [1.0 / v for v in vs]
        return ready[h]

    def scores_of(h, cs):
        keys, q = prepared(h)[:2]
        return lax.dot_general(keys, q[cs], (((1,), (1,)), ((), ())), preferred_element_type=F32)

    def softmax(h, cs, scores):
        ks, lv = prepared(h)[2:4]
        parts = [scores[b * block : (b + 1) * block] * ks[b] for b in range(count)]
        top = functools.reduce(jnp.maximum, [jnp.max(p, axis=0, keepdims=True) for p in parts])
        factor = None
        if old is not None:
            before = old[0][h : h + 1, cs]
            top = jnp.maximum(top, before)
            factor = jnp.exp2(before - top)
        weights = [jnp.exp2(parts[b] - (top - lv[b])).astype(BF16) for b in range(count)]
        return jnp.concatenate(weights, axis=0), top, factor

    def finish(h, cs, weights, top, factor):
        iv = prepared(h)[4]
        values = jnp.concatenate([stacked((heads + h) * tokens), ones], axis=1)
        acc = lax.dot_general(values, weights, (((0,), (0,)), ((), ())), preferred_element_type=F32)
        total = functools.reduce(jnp.add, [acc[width + b : width + b + 1] * iv[b] for b in range(count)])
        acc = acc[:width]
        if factor is not None:
            total = total + old[1][h : h + 1, cs] * factor
            acc = acc + old[2][h, :, cs] * factor
        put(h, cs, acc, top, total)

    scores = scores_of(*units[0])
    waiting = None
    for i, (h, cs) in enumerate(units):
        following = scores_of(*units[i + 1]) if i + 1 < len(units) else None
        done = softmax(h, cs, scores)
        if waiting is not None:
            finish(*waiting)
        waiting = (h, cs) + done
        scores = following
    finish(*waiting)


def prepare_kernel(heads, group, length_hbm, q_ref, qh_ref, *refs):
    masks, (length_ref, length_sem, q_buf, q_sem) = refs[:-4], refs[-4:]
    tokens, _, width = q_ref.shape
    rows, block, pair = tokens * group, 2 * tokens, 2 * group
    copies = [
        pltpu.make_async_copy(q_ref.at[:, pl.ds(g * pair, pair), :], q_buf.at[g], q_sem.at[g]) for g in range(heads // 2)
    ]
    lengths = pltpu.make_async_copy(length_hbm, length_ref, length_sem)
    lengths.start()
    for copy in copies:
        copy.start()
    chip, core = lax.axis_index("ctx"), lax.axis_index("tp")
    even = chip % 2 == 0
    position = chip * block + core * tokens + lax.broadcasted_iota(jnp.int32, (8, width), 1)

    def later(i, carry):
        start, end = carry
        end = end + length_ref[i]
        return jnp.where(position >= end, end, start), end

    lengths.wait()
    start, _ = lax.fori_loop(0, length_ref.shape[0], later, (jnp.zeros_like(position), jnp.int32(0)))
    start, position = start[:1], position[:1]
    i = lax.broadcasted_iota(jnp.int32, (block, width), 0)
    offset = jnp.where(i < tokens, core * tokens + i, (1 - core) * tokens + i - tokens)
    for b, back in enumerate((0, 4, jnp.where(even, 1, 3), jnp.where(even, 3, 1), 2)):
        key = (chip - back) * block + (i if b == GATHERED else offset)
        masks[b][...] = jnp.where((key >= start) & (key <= position), 0.0, NEG).astype(BF16)
    for h in range(heads):
        if h % 2 == 0:
            copies[h // 2].wait()
        qh_ref[h] = q_buf[h // 2][:, (h % 2) * group : (h % 2 + 1) * group, :].reshape(rows, width)


def early_kernel(count, heads, group, qh_ref, *refs):
    masks, mine, sibling = refs[:count], refs[count : 2 * count], refs[2 * count : 3 * count]
    acc_ref, top_ref, sum_ref = refs[3 * count :]
    _, rows, width = qh_ref.shape
    tokens = rows // group
    scale = scales_of(mine, sibling, heads, tokens, lax.axis_index("tp") == 0)
    mask = jnp.concatenate([ref[...] for ref in masks], axis=0)

    def put(h, cs, acc, top, total):
        acc_ref[h, :, cs] = acc
        top_ref[h : h + 1, cs] = top
        sum_ref[h : h + 1, cs] = total

    attend_blocks(lambda h: qh_ref[h], put, mask, mine, sibling, scale, heads, tokens, group, width, None)


def middle_kernel(heads, group, qh_ref, mask_ref, acc_ref, top_ref, sum_ref, both_ref, acc_out, top_out, sum_out):
    _, rows, width = qh_ref.shape
    tokens = rows // group
    size = both_ref.shape[0] // 2
    mine, sibling = [both_ref.at[:size]], [both_ref.at[size:]]
    scale = scales_of(mine, sibling, heads, tokens, True)

    def put(h, cs, acc, top, total):
        acc_out[h, :, cs] = acc
        top_out[h : h + 1, cs] = top
        sum_out[h : h + 1, cs] = total

    attend_blocks(
        lambda h: qh_ref[h], put, mask_ref[...], mine, sibling, scale, heads, tokens, group, width, (top_ref, sum_ref, acc_ref)
    )


def last_kernel(count, heads, group, qh_ref, acc_ref, top_ref, sum_ref, *refs):
    masks, mine, sibling = refs[:count], refs[count : 2 * count], refs[2 * count : 3 * count]
    out_ref, o_buf, o_sem = refs[3 * count :]
    _, rows, width = qh_ref.shape
    tokens, pair = rows // group, 2 * group
    scale = scales_of(mine, sibling, heads, tokens, lax.axis_index("tp") == 0)
    mask = jnp.concatenate([ref[...] for ref in masks], axis=0)
    copies = []

    def put(h, cs, acc, top, total):
        out = (acc / total).T.astype(BF16)
        span = slice(cs.start // group, cs.stop // group)
        o_buf[h // 2, span, (h % 2) * group : (h % 2 + 1) * group, :] = out.reshape(span.stop - span.start, group, width)
        if h % 2 == 1 and cs.stop == rows:
            g = h // 2
            copies.append(pltpu.make_async_copy(o_buf.at[g], out_ref.at[:, pl.ds(g * pair, pair), :], o_sem.at[g]))
            copies[-1].start()

    attend_blocks(
        lambda h: qh_ref[h], put, mask, mine, sibling, scale, heads, tokens, group, width, (top_ref, sum_ref, acc_ref)
    )
    for copy in copies:
        copy.wait()


def cost(tokens, q_heads, width, blocks):
    work = tokens * q_heads * blocks * 2 * tokens
    return pl.CostEstimate(flops=4 * work * width, bytes_accessed=2 * tokens * q_heads * width, transcendentals=work)


def prepare(queries, lengths, heads, blocks=5):
    tokens, q_heads, width = queries.shape
    group = q_heads // heads
    out = [((heads, tokens * group, width), BF16)] + [((2 * tokens, width), BF16)] * blocks
    qh, *masks = pl.pallas_call(
        functools.partial(prepare_kernel, heads, group),
        out_shape=[jax.ShapeDtypeStruct(*x) for x in out],
        in_specs=[pl.BlockSpec(memory_space=HBM)] * 2,
        out_specs=[WHOLE] * (1 + blocks),
        scratch_shapes=[
            pltpu.SMEM(lengths.shape, lengths.dtype),
            pltpu.SemaphoreType.DMA,
            pltpu.VMEM((heads // 2, tokens, 2 * group, width), BF16),
            pltpu.SemaphoreType.DMA((heads // 2,)),
        ],
        compiler_params=pltpu.CompilerParams(vmem_limit_bytes=24 * 2**20),
        name="prepare",
    )(*(pltpu.with_memory_space_constraint(x, HBM) for x in (lengths, queries)))
    return qh, masks


def early(qh, masks, mine, sibling):
    heads, rows, width = qh.shape
    count, tokens = len(mine), masks[0].shape[0] // 2
    group = rows // tokens
    shape = jax.ShapeDtypeStruct
    return pl.pallas_call(
        functools.partial(early_kernel, count, heads, group),
        out_shape=[shape((heads, width, rows), F32), shape((heads, rows), F32), shape((heads, rows), F32)],
        in_specs=[WHOLE] * (1 + 3 * count),
        out_specs=[WHOLE] * 3,
        compiler_params=pltpu.CompilerParams(vmem_limit_bytes=24 * 2**20),
        cost_estimate=cost(tokens, heads * group, width, count),
        name="early",
    )(qh, *masks, *mine, *sibling)


def middle(state, qh, mask, both):
    heads, rows, width = qh.shape
    tokens = mask.shape[0] // 2
    group = rows // tokens
    return pl.pallas_call(
        functools.partial(middle_kernel, heads, group),
        out_shape=[jax.ShapeDtypeStruct(x.shape, x.dtype) for x in state],
        in_specs=[WHOLE] * 6,
        out_specs=[WHOLE] * 3,
        compiler_params=pltpu.CompilerParams(vmem_limit_bytes=24 * 2**20),
        cost_estimate=cost(tokens, heads * group, width, 1),
        name="middle",
    )(qh, mask, *state, both)


def last(state, qh, masks, mine, sibling):
    heads, rows, width = qh.shape
    count, tokens = len(mine), masks[0].shape[0] // 2
    group = rows // tokens
    return pl.pallas_call(
        functools.partial(last_kernel, count, heads, group),
        out_shape=jax.ShapeDtypeStruct((tokens, heads * group, width), BF16),
        in_specs=[WHOLE] * (4 + 3 * count),
        out_specs=pl.BlockSpec(memory_space=HBM),
        scratch_shapes=[
            pltpu.VMEM((heads // 2, tokens, 2 * group, width), BF16),
            pltpu.SemaphoreType.DMA((heads // 2,)),
        ],
        compiler_params=pltpu.CompilerParams(vmem_limit_bytes=24 * 2**20),
        cost_estimate=cost(tokens, heads * group, width, count),
        name="last",
    )(qh, *state, *masks, *mine, *sibling)


def shards(queries, keys, values, key_scales, value_scales, lengths):
    tokens, heads, _ = keys.shape
    ranks = lax.axis_size("ctx")
    c = lax.axis_index("ctx")
    own = pack(keys, values, key_scales, value_scales)

    def send(value, target):
        pairs = [(source, target(source)) for source in range(ranks)]
        return lax.ppermute(value, "ctx", [(i, j) for i, j in pairs if 0 <= j < ranks])

    def swap(value):
        return lax.ppermute(value, "tp", [(0, 1), (1, 0)])

    k = c % 4
    even = k % 2 == 0
    from_z = send(own, lambda i: (i + 4) % ranks)
    from_d = send(own, lambda i: i + (3 if i % 2 == 0 else 1))
    qh, masks = prepare(queries, lengths, heads)
    from_z, masks[0] = lax.optimization_barrier((from_z, masks[0]))
    from_x = send(jnp.where(even, own, from_z), lambda i: i ^ 1)
    from_y = send(jnp.where(k < 2, own, from_z), lambda i: i ^ 2)
    acc, top, total = early(qh, masks[:2], [own, from_z], [swap(own), swap(from_z)])
    from_d, top = lax.optimization_barrier((from_d, top))
    both_d = lax.all_gather(from_d, "tp", axis=0, tiled=True)
    acc, top, total = middle((acc, top, total), qh, masks[GATHERED], both_d)
    from_x, from_y, top = lax.optimization_barrier((from_x, from_y, top))
    return last((acc, top, total), qh, masks[3:], [from_x, from_y], [swap(from_x), swap(from_y)])


def solution(mesh):
    both = P(("ctx", "tp"), None, None)
    return jax.shard_map(
        shards,
        mesh=mesh,
        in_specs=(both, both, both, P("ctx", "tp"), P("ctx", "tp"), P()),
        out_specs=both,
        check_vma=False,
    )
```

```python
import functools
import math

import jax
import jax.numpy as jnp
from jax import lax
from jax.experimental import pallas as pl
from jax.experimental.pallas import tpu as pltpu
from jax.sharding import PartitionSpec as P

NEG = -1e30
VMEM = pltpu.MemorySpace.VMEM
HBM = pltpu.MemorySpace.HBM
F32 = jnp.float32
BF16 = jnp.bfloat16
WHOLE = pl.BlockSpec(memory_space=VMEM)
SCALE_ROWS = 16
CHUNK = 256
GATHERED = 2


def pack_kernel(k_ref, v_ref, ks_ref, vs_ref, out_ref, rows_ref):
    tokens, heads, width = k_ref.shape
    for part, ref in enumerate((k_ref, v_ref)):
        rows_ref[part] = ref[...].astype(F32).reshape(tokens * heads, width)
        for head in range(heads):
            start = (part * heads + head) * tokens
            rows = rows_ref[part, pl.ds(head, tokens, stride=heads), :]
            out_ref[start : start + tokens, :] = rows.astype(out_ref.dtype)
    held = ks_ref.shape[1]
    row = lax.broadcasted_iota(jnp.int32, (SCALE_ROWS, held), 0)
    col = lax.broadcasted_iota(jnp.int32, (SCALE_ROWS, held), 1)
    k_scale = jnp.broadcast_to(ks_ref[...].astype(F32), row.shape)
    v_scale = jnp.broadcast_to(vs_ref[...].astype(F32), row.shape)
    both = jnp.where(row == col, k_scale, 0.0) + jnp.where(row == col + held, v_scale, 0.0)
    both = jnp.broadcast_to(jnp.sum(both, axis=1, keepdims=True), (SCALE_ROWS, width))
    out_ref[2 * heads * tokens :, :] = both.astype(out_ref.dtype)


def pack(keys, values, key_scales, value_scales):
    tokens, heads, width = keys.shape
    args = [pltpu.with_memory_space_constraint(x, HBM) for x in (keys, values, key_scales, value_scales)]
    return pl.pallas_call(
        pack_kernel,
        out_shape=jax.ShapeDtypeStruct((2 * heads * tokens + SCALE_ROWS, width), keys.dtype),
        grid=(1,),
        in_specs=[pl.BlockSpec(x.shape, lambda i, n=x.ndim: (0,) * n) for x in (keys, values, key_scales, value_scales)],
        out_specs=WHOLE,
        scratch_shapes=[pltpu.VMEM((2, tokens * heads, width), F32)],
        compiler_params=pltpu.CompilerParams(vmem_limit_bytes=8 * 2**20),
        name="pack",
    )(*args)


def scales_of(mine, sibling, heads, tokens, first):
    low = 2 * heads * tokens
    out = []
    for m, s in zip(mine, sibling):
        a, z = m[low:, :].astype(F32), s[low:, :].astype(F32)
        a, z = jnp.where(a > 0, a, 1.0), jnp.where(z > 0, z, 1.0)
        out.append((jnp.where(first, a, z), jnp.where(first, z, a)))
    return out


def attend_blocks(get_q, put, mask, mine, sibling, scale, heads, tokens, group, width, old):
    count = len(mine)
    block = 2 * tokens
    rows = tokens * group
    local = heads // 2
    chunk = min(CHUNK, rows)
    row_token = lax.broadcasted_iota(jnp.int32, (rows, width), 0) // group
    one_hot = jnp.where(row_token == lax.broadcasted_iota(jnp.int32, (rows, width), 1), 1.0, 0.0).astype(BF16)
    of_key = lax.broadcasted_iota(jnp.int32, (block * count, width), 0) // block
    ones = jnp.where(of_key == lax.broadcasted_iota(jnp.int32, (block * count, width), 1), 1.0, 0.0).astype(BF16)
    units = [(h, slice(r, r + chunk)) for h in range(heads) for r in range(0, rows, chunk)]
    ready = {}

    def stacked(at):
        return jnp.concatenate([r[at : at + tokens, :] for b in range(count) for r in (mine[b], sibling[b])], axis=0)

    def wide(x):
        return jnp.concatenate([x] * (chunk // width), axis=1)

    def prepared(h):
        if h not in ready:
            keys = jnp.concatenate([stacked(h * tokens), mask], axis=1)
            q = jnp.concatenate([get_q(h), one_hot], axis=1)
            part, at = h // local, h % local
            ks = [wide(s[part][at : at + 1, :] * (math.log2(math.e) / math.sqrt(width))) for s in scale]
            vs = [wide(s[part][local + at : local + at + 1, :]) for s in scale]
            ready[h] = keys, q, ks, [jnp.log2(v) for v in vs], [1.0 / v for v in vs]
        return ready[h]

    def scores_of(h, cs):
        keys, q = prepared(h)[:2]
        return lax.dot_general(keys, q[cs], (((1,), (1,)), ((), ())), preferred_element_type=F32)

    def softmax(h, cs, scores):
        ks, lv = prepared(h)[2:4]
        parts = [scores[b * block : (b + 1) * block] * ks[b] for b in range(count)]
        top = functools.reduce(jnp.maximum, [jnp.max(p, axis=0, keepdims=True) for p in parts])
        factor = None
        if old is not None:
            before = old[0][h : h + 1, cs]
            top = jnp.maximum(top, before)
            factor = jnp.exp2(before - top)
        weights = [jnp.exp2(parts[b] - (top - lv[b])).astype(BF16) for b in range(count)]
        return jnp.concatenate(weights, axis=0), top, factor

    def finish(h, cs, weights, top, factor):
        iv = prepared(h)[4]
        values = jnp.concatenate([stacked((heads + h) * tokens), ones], axis=1)
        acc = lax.dot_general(values, weights, (((0,), (0,)), ((), ())), preferred_element_type=F32)
        total = functools.reduce(jnp.add, [acc[width + b : width + b + 1] * iv[b] for b in range(count)])
        acc = acc[:width]
        if factor is not None:
            total = total + old[1][h : h + 1, cs] * factor
            acc = acc + old[2][h, :, cs] * factor
        put(h, cs, acc, top, total)

    scores = scores_of(*units[0])
    waiting = None
    for i, (h, cs) in enumerate(units):
        following = scores_of(*units[i + 1]) if i + 1 < len(units) else None
        done = softmax(h, cs, scores)
        if waiting is not None:
            finish(*waiting)
        waiting = (h, cs) + done
        scores = following
    finish(*waiting)


def prepare_kernel(heads, group, length_hbm, q_ref, qh_ref, *refs):
    masks, (length_ref, length_sem, q_buf, q_sem) = refs[:-4], refs[-4:]
    tokens, _, width = q_ref.shape
    rows, block, pair = tokens * group, 2 * tokens, 2 * group
    copies = [
        pltpu.make_async_copy(q_ref.at[:, pl.ds(g * pair, pair), :], q_buf.at[g], q_sem.at[g]) for g in range(heads // 2)
    ]
    lengths = pltpu.make_async_copy(length_hbm, length_ref, length_sem)
    lengths.start()
    for copy in copies:
        copy.start()
    chip, core = lax.axis_index("ctx"), lax.axis_index("tp")
    even = chip % 2 == 0
    position = chip * block + core * tokens + lax.broadcasted_iota(jnp.int32, (8, width), 1)

    def later(i, carry):
        start, end = carry
        end = end + length_ref[i]
        return jnp.where(position >= end, end, start), end

    lengths.wait()
    start, _ = lax.fori_loop(0, length_ref.shape[0], later, (jnp.zeros_like(position), jnp.int32(0)))
    start, position = start[:1], position[:1]
    i = lax.broadcasted_iota(jnp.int32, (block, width), 0)
    offset = jnp.where(i < tokens, core * tokens + i, (1 - core) * tokens + i - tokens)
    for b, back in enumerate((0, 4, jnp.where(even, 1, 3), jnp.where(even, 3, 1), 2)):
        key = (chip - back) * block + (i if b == GATHERED else offset)
        masks[b][...] = jnp.where((key >= start) & (key <= position), 0.0, NEG).astype(BF16)
    for h in range(heads):
        if h % 2 == 0:
            copies[h // 2].wait()
        qh_ref[h] = q_buf[h // 2][:, (h % 2) * group : (h % 2 + 1) * group, :].reshape(rows, width)


def early_kernel(count, heads, group, qh_ref, *refs):
    masks, mine, sibling = refs[:count], refs[count : 2 * count], refs[2 * count : 3 * count]
    acc_ref, top_ref, sum_ref = refs[3 * count :]
    _, rows, width = qh_ref.shape
    tokens = rows // group
    scale = scales_of(mine, sibling, heads, tokens, lax.axis_index("tp") == 0)
    mask = jnp.concatenate([ref[...] for ref in masks], axis=0)

    def put(h, cs, acc, top, total):
        acc_ref[h, :, cs] = acc
        top_ref[h : h + 1, cs] = top
        sum_ref[h : h + 1, cs] = total

    attend_blocks(lambda h: qh_ref[h], put, mask, mine, sibling, scale, heads, tokens, group, width, None)


def middle_kernel(heads, group, qh_ref, mask_ref, acc_ref, top_ref, sum_ref, both_ref, acc_out, top_out, sum_out):
    _, rows, width = qh_ref.shape
    tokens = rows // group
    size = both_ref.shape[0] // 2
    mine, sibling = [both_ref.at[:size]], [both_ref.at[size:]]
    scale = scales_of(mine, sibling, heads, tokens, True)

    def put(h, cs, acc, top, total):
        acc_out[h, :, cs] = acc
        top_out[h : h + 1, cs] = top
        sum_out[h : h + 1, cs] = total

    attend_blocks(
        lambda h: qh_ref[h], put, mask_ref[...], mine, sibling, scale, heads, tokens, group, width, (top_ref, sum_ref, acc_ref)
    )


def last_kernel(count, heads, group, qh_ref, acc_ref, top_ref, sum_ref, *refs):
    masks, mine, sibling = refs[:count], refs[count : 2 * count], refs[2 * count : 3 * count]
    out_ref, o_buf, o_sem = refs[3 * count :]
    _, rows, width = qh_ref.shape
    tokens, pair = rows // group, 2 * group
    scale = scales_of(mine, sibling, heads, tokens, lax.axis_index("tp") == 0)
    mask = jnp.concatenate([ref[...] for ref in masks], axis=0)
    copies = []

    def put(h, cs, acc, top, total):
        out = (acc * (1.0 / total)).astype(BF16).T
        span = slice(cs.start // group, cs.stop // group)
        o_buf[h // 2, span, (h % 2) * group : (h % 2 + 1) * group, :] = out.reshape(span.stop - span.start, group, width)
        if h % 2 == 1 and cs.stop == rows:
            g = h // 2
            copies.append(pltpu.make_async_copy(o_buf.at[g], out_ref.at[:, pl.ds(g * pair, pair), :], o_sem.at[g]))
            copies[-1].start()

    attend_blocks(
        lambda h: qh_ref[h], put, mask, mine, sibling, scale, heads, tokens, group, width, (top_ref, sum_ref, acc_ref)
    )
    for copy in copies:
        copy.wait()


def cost(tokens, q_heads, width, blocks):
    work = tokens * q_heads * blocks * 2 * tokens
    return pl.CostEstimate(flops=4 * work * width, bytes_accessed=2 * tokens * q_heads * width, transcendentals=work)


def prepare(queries, lengths, heads, blocks=5):
    tokens, q_heads, width = queries.shape
    group = q_heads // heads
    out = [((heads, tokens * group, width), BF16)] + [((2 * tokens, width), BF16)] * blocks
    qh, *masks = pl.pallas_call(
        functools.partial(prepare_kernel, heads, group),
        out_shape=[jax.ShapeDtypeStruct(*x) for x in out],
        in_specs=[pl.BlockSpec(memory_space=HBM)] * 2,
        out_specs=[WHOLE] * (1 + blocks),
        scratch_shapes=[
            pltpu.SMEM(lengths.shape, lengths.dtype),
            pltpu.SemaphoreType.DMA,
            pltpu.VMEM((heads // 2, tokens, 2 * group, width), BF16),
            pltpu.SemaphoreType.DMA((heads // 2,)),
        ],
        compiler_params=pltpu.CompilerParams(vmem_limit_bytes=24 * 2**20),
        name="prepare",
    )(*(pltpu.with_memory_space_constraint(x, HBM) for x in (lengths, queries)))
    return qh, masks


def early(qh, masks, mine, sibling):
    heads, rows, width = qh.shape
    count, tokens = len(mine), masks[0].shape[0] // 2
    group = rows // tokens
    shape = jax.ShapeDtypeStruct
    return pl.pallas_call(
        functools.partial(early_kernel, count, heads, group),
        out_shape=[shape((heads, width, rows), F32), shape((heads, rows), F32), shape((heads, rows), F32)],
        in_specs=[WHOLE] * (1 + 3 * count),
        out_specs=[WHOLE] * 3,
        compiler_params=pltpu.CompilerParams(vmem_limit_bytes=24 * 2**20),
        cost_estimate=cost(tokens, heads * group, width, count),
        name="early",
    )(qh, *masks, *mine, *sibling)


def middle(state, qh, mask, both):
    heads, rows, width = qh.shape
    tokens = mask.shape[0] // 2
    group = rows // tokens
    return pl.pallas_call(
        functools.partial(middle_kernel, heads, group),
        out_shape=[jax.ShapeDtypeStruct(x.shape, x.dtype) for x in state],
        in_specs=[WHOLE] * 6,
        out_specs=[WHOLE] * 3,
        compiler_params=pltpu.CompilerParams(vmem_limit_bytes=24 * 2**20),
        cost_estimate=cost(tokens, heads * group, width, 1),
        name="middle",
    )(qh, mask, *state, both)


def last(state, qh, masks, mine, sibling):
    heads, rows, width = qh.shape
    count, tokens = len(mine), masks[0].shape[0] // 2
    group = rows // tokens
    return pl.pallas_call(
        functools.partial(last_kernel, count, heads, group),
        out_shape=jax.ShapeDtypeStruct((tokens, heads * group, width), BF16),
        in_specs=[WHOLE] * (4 + 3 * count),
        out_specs=pl.BlockSpec(memory_space=HBM),
        scratch_shapes=[
            pltpu.VMEM((heads // 2, tokens, 2 * group, width), BF16),
            pltpu.SemaphoreType.DMA((heads // 2,)),
        ],
        compiler_params=pltpu.CompilerParams(vmem_limit_bytes=24 * 2**20),
        cost_estimate=cost(tokens, heads * group, width, count),
        name="last",
    )(qh, *state, *masks, *mine, *sibling)


def shards(queries, keys, values, key_scales, value_scales, lengths):
    tokens, heads, _ = keys.shape
    ranks = lax.axis_size("ctx")
    c = lax.axis_index("ctx")
    own = pack(keys, values, key_scales, value_scales)

    def send(value, target):
        pairs = [(source, target(source)) for source in range(ranks)]
        return lax.ppermute(value, "ctx", [(i, j) for i, j in pairs if 0 <= j < ranks])

    def swap(value):
        return lax.ppermute(value, "tp", [(0, 1), (1, 0)])

    k = c % 4
    even = k % 2 == 0
    from_z = send(own, lambda i: (i + 4) % ranks)
    from_d = send(own, lambda i: i + (3 if i % 2 == 0 else 1))
    qh, masks = prepare(queries, lengths, heads)
    from_z, masks[0] = lax.optimization_barrier((from_z, masks[0]))
    from_x = send(jnp.where(even, own, from_z), lambda i: i ^ 1)
    from_y = send(jnp.where(k < 2, own, from_z), lambda i: i ^ 2)
    acc, top, total = early(qh, masks[:2], [own, from_z], [swap(own), swap(from_z)])
    from_d, top = lax.optimization_barrier((from_d, top))
    both_d = lax.all_gather(from_d, "tp", axis=0, tiled=True)
    acc, top, total = middle((acc, top, total), qh, masks[GATHERED], both_d)
    from_x, from_y, top = lax.optimization_barrier((from_x, from_y, top))
    return last((acc, top, total), qh, masks[3:], [from_x, from_y], [swap(from_x), swap(from_y)])


def solution(mesh):
    both = P(("ctx", "tp"), None, None)
    return jax.shard_map(
        shards,
        mesh=mesh,
        in_specs=(both, both, both, P("ctx", "tp"), P("ctx", "tp"), P()),
        out_specs=both,
        check_vma=False,
    )
```

```python
import functools
import math

import jax
import jax.numpy as jnp
from jax import lax
from jax.experimental import pallas as pl
from jax.experimental.pallas import tpu as pltpu
from jax.sharding import PartitionSpec as P

NEG = -1e30
VMEM = pltpu.MemorySpace.VMEM
HBM = pltpu.MemorySpace.HBM
F32 = jnp.float32
BF16 = jnp.bfloat16
WHOLE = pl.BlockSpec(memory_space=VMEM)
SCALE_ROWS = 16
CHUNK = 256
GATHERED = 2


def pack_kernel(k_ref, v_ref, ks_ref, vs_ref, out_ref, rows_ref):
    tokens, heads, width = k_ref.shape
    for part, ref in enumerate((k_ref, v_ref)):
        rows_ref[part] = ref[...].astype(F32).reshape(tokens * heads, width)
        for head in range(heads):
            start = (part * heads + head) * tokens
            rows = rows_ref[part, pl.ds(head, tokens, stride=heads), :]
            out_ref[start : start + tokens, :] = rows.astype(out_ref.dtype)
    held = ks_ref.shape[1]
    row = lax.broadcasted_iota(jnp.int32, (SCALE_ROWS, held), 0)
    col = lax.broadcasted_iota(jnp.int32, (SCALE_ROWS, held), 1)
    k_scale = jnp.broadcast_to(ks_ref[...].astype(F32), row.shape)
    v_scale = jnp.broadcast_to(vs_ref[...].astype(F32), row.shape)
    both = jnp.where(row == col, k_scale, 0.0) + jnp.where(row == col + held, v_scale, 0.0)
    both = jnp.broadcast_to(jnp.sum(both, axis=1, keepdims=True), (SCALE_ROWS, width))
    out_ref[2 * heads * tokens :, :] = both.astype(out_ref.dtype)


def pack(keys, values, key_scales, value_scales):
    tokens, heads, width = keys.shape
    args = [pltpu.with_memory_space_constraint(x, HBM) for x in (keys, values, key_scales, value_scales)]
    return pl.pallas_call(
        pack_kernel,
        out_shape=jax.ShapeDtypeStruct((2 * heads * tokens + SCALE_ROWS, width), keys.dtype),
        grid=(1,),
        in_specs=[pl.BlockSpec(x.shape, lambda i, n=x.ndim: (0,) * n) for x in (keys, values, key_scales, value_scales)],
        out_specs=WHOLE,
        scratch_shapes=[pltpu.VMEM((2, tokens * heads, width), F32)],
        compiler_params=pltpu.CompilerParams(vmem_limit_bytes=8 * 2**20),
        name="pack",
    )(*args)


def scales_of(mine, sibling, heads, tokens, first):
    low = 2 * heads * tokens
    out = []
    for m, s in zip(mine, sibling):
        a, z = m[low:, :].astype(F32), s[low:, :].astype(F32)
        a, z = jnp.where(a > 0, a, 1.0), jnp.where(z > 0, z, 1.0)
        out.append((jnp.where(first, a, z), jnp.where(first, z, a)))
    return out


def attend_blocks(get_q, put, mask, mine, sibling, scale, heads, tokens, group, width, old):
    count = len(mine)
    block = 2 * tokens
    rows = tokens * group
    local = heads // 2
    chunk = min(CHUNK, rows)
    row_token = lax.broadcasted_iota(jnp.int32, (rows, width), 0) // group
    one_hot = jnp.where(row_token == lax.broadcasted_iota(jnp.int32, (rows, width), 1), 1.0, 0.0).astype(BF16)
    of_key = lax.broadcasted_iota(jnp.int32, (block * count, width), 0) // block
    ones = jnp.where(of_key == lax.broadcasted_iota(jnp.int32, (block * count, width), 1), 1.0, 0.0).astype(BF16)
    units = [(h, slice(r, r + chunk)) for h in range(heads) for r in range(0, rows, chunk)]
    ready = {}

    def stacked(at):
        return jnp.concatenate([r[at : at + tokens, :] for b in range(count) for r in (mine[b], sibling[b])], axis=0)

    def wide(x):
        return jnp.concatenate([x] * (chunk // width), axis=1)

    def prepared(h):
        if h not in ready:
            keys = jnp.concatenate([stacked(h * tokens), mask], axis=1)
            q = jnp.concatenate([get_q(h), one_hot], axis=1)
            part, at = h // local, h % local
            ks = [wide(s[part][at : at + 1, :] * (math.log2(math.e) / math.sqrt(width))) for s in scale]
            vs = [wide(s[part][local + at : local + at + 1, :]) for s in scale]
            ready[h] = keys, q, ks, [jnp.log2(v) for v in vs], [1.0 / v for v in vs]
        return ready[h]

    def scores_of(h, cs):
        keys, q = prepared(h)[:2]
        return lax.dot_general(keys, q[cs], (((1,), (1,)), ((), ())), preferred_element_type=F32)

    def softmax(h, cs, scores):
        ks, lv = prepared(h)[2:4]
        parts = [scores[b * block : (b + 1) * block] * ks[b] for b in range(count)]
        top = functools.reduce(jnp.maximum, [jnp.max(p, axis=0, keepdims=True) for p in parts])
        factor = None
        if old is not None:
            before = old[0][h : h + 1, cs]
            top = jnp.maximum(top, before)
            factor = jnp.exp2(before - top)
        weights = [jnp.exp2(parts[b] - (top - lv[b])).astype(BF16) for b in range(count)]
        return jnp.concatenate(weights, axis=0), top, factor

    def finish(h, cs, weights, top, factor):
        iv = prepared(h)[4]
        values = jnp.concatenate([stacked((heads + h) * tokens), ones], axis=1)
        acc = lax.dot_general(values, weights, (((0,), (0,)), ((), ())), preferred_element_type=F32)
        total = functools.reduce(jnp.add, [acc[width + b : width + b + 1] * iv[b] for b in range(count)])
        acc = acc[:width]
        if factor is not None:
            total = total + old[1][h : h + 1, cs] * factor
            acc = acc + old[2][h, :, cs] * factor
        put(h, cs, acc, top, total)

    scores = scores_of(*units[0])
    waiting = None
    for i, (h, cs) in enumerate(units):
        following = scores_of(*units[i + 1]) if i + 1 < len(units) else None
        done = softmax(h, cs, scores)
        if waiting is not None:
            finish(*waiting)
        waiting = (h, cs) + done
        scores = following
    finish(*waiting)


def prepare_kernel(heads, group, length_hbm, q_ref, qh_ref, *refs):
    masks, (length_ref, length_sem, q_buf, q_sem) = refs[:-4], refs[-4:]
    tokens, _, width = q_ref.shape
    rows, block, pair = tokens * group, 2 * tokens, 2 * group
    copies = [
        pltpu.make_async_copy(q_ref.at[:, pl.ds(g * pair, pair), :], q_buf.at[g], q_sem.at[g]) for g in range(heads // 2)
    ]
    lengths = pltpu.make_async_copy(length_hbm, length_ref, length_sem)
    lengths.start()
    for copy in copies:
        copy.start()
    chip, core = lax.axis_index("ctx"), lax.axis_index("tp")
    even = chip % 2 == 0
    position = chip * block + core * tokens + lax.broadcasted_iota(jnp.int32, (8, width), 1)

    def later(i, carry):
        start, end = carry
        end = end + length_ref[i]
        return jnp.where(position >= end, end, start), end

    lengths.wait()
    start, _ = lax.fori_loop(0, length_ref.shape[0], later, (jnp.zeros_like(position), jnp.int32(0)))
    start, position = start[:1], position[:1]
    i = lax.broadcasted_iota(jnp.int32, (block, width), 0)
    offset = jnp.where(i < tokens, core * tokens + i, (1 - core) * tokens + i - tokens)
    for b, back in enumerate((0, 4, jnp.where(even, 1, 3), jnp.where(even, 3, 1), 2)):
        key = (chip - back) * block + (i if b == GATHERED else offset)
        masks[b][...] = jnp.where((key >= start) & (key <= position), 0.0, NEG).astype(BF16)
    for h in range(heads):
        if h % 2 == 0:
            copies[h // 2].wait()
        qh_ref[h] = q_buf[h // 2][:, (h % 2) * group : (h % 2 + 1) * group, :].reshape(rows, width)


def early_kernel(count, heads, group, qh_ref, *refs):
    masks, mine, sibling = refs[:count], refs[count : 2 * count], refs[2 * count : 3 * count]
    acc_ref, top_ref, sum_ref = refs[3 * count :]
    _, rows, width = qh_ref.shape
    tokens = rows // group
    scale = scales_of(mine, sibling, heads, tokens, lax.axis_index("tp") == 0)
    mask = jnp.concatenate([ref[...] for ref in masks], axis=0)

    def put(h, cs, acc, top, total):
        acc_ref[h, :, cs] = acc
        top_ref[h : h + 1, cs] = top
        sum_ref[h : h + 1, cs] = total

    attend_blocks(lambda h: qh_ref[h], put, mask, mine, sibling, scale, heads, tokens, group, width, None)


def middle_kernel(heads, group, qh_ref, mask_ref, acc_ref, top_ref, sum_ref, both_ref, acc_out, top_out, sum_out):
    _, rows, width = qh_ref.shape
    tokens = rows // group
    size = both_ref.shape[0] // 2
    mine, sibling = [both_ref.at[:size]], [both_ref.at[size:]]
    scale = scales_of(mine, sibling, heads, tokens, True)

    def put(h, cs, acc, top, total):
        acc_out[h, :, cs] = acc
        top_out[h : h + 1, cs] = top
        sum_out[h : h + 1, cs] = total

    attend_blocks(
        lambda h: qh_ref[h], put, mask_ref[...], mine, sibling, scale, heads, tokens, group, width, (top_ref, sum_ref, acc_ref)
    )


def last_kernel(count, heads, group, qh_ref, acc_ref, top_ref, sum_ref, *refs):
    masks, mine, sibling = refs[:count], refs[count : 2 * count], refs[2 * count : 3 * count]
    out_ref, o_buf, o_sem = refs[3 * count :]
    _, rows, width = qh_ref.shape
    tokens, pair = rows // group, 2 * group
    scale = scales_of(mine, sibling, heads, tokens, lax.axis_index("tp") == 0)
    mask = jnp.concatenate([ref[...] for ref in masks], axis=0)
    copies = []

    def put(h, cs, acc, top, total):
        out = (acc * (1.0 / total)).astype(BF16).T
        span = slice(cs.start // group, cs.stop // group)
        o_buf[h // 2, span, (h % 2) * group : (h % 2 + 1) * group, :] = out.reshape(span.stop - span.start, group, width)
        if h % 2 == 1 and cs.stop == rows:
            g = h // 2
            copies.append(pltpu.make_async_copy(o_buf.at[g], out_ref.at[:, pl.ds(g * pair, pair), :], o_sem.at[g]))
            copies[-1].start()

    attend_blocks(
        lambda h: qh_ref[h], put, mask, mine, sibling, scale, heads, tokens, group, width, (top_ref, sum_ref, acc_ref)
    )
    for copy in copies:
        copy.wait()


def cost(tokens, q_heads, width, blocks):
    work = tokens * q_heads * blocks * 2 * tokens
    return pl.CostEstimate(flops=4 * work * width, bytes_accessed=2 * tokens * q_heads * width, transcendentals=work)


def prepare(queries, lengths, heads, blocks=5):
    tokens, q_heads, width = queries.shape
    group = q_heads // heads
    out = [((heads, tokens * group, width), BF16)] + [((2 * tokens, width), BF16)] * blocks
    qh, *masks = pl.pallas_call(
        functools.partial(prepare_kernel, heads, group),
        out_shape=[jax.ShapeDtypeStruct(*x) for x in out],
        in_specs=[pl.BlockSpec(memory_space=HBM)] * 2,
        out_specs=[WHOLE] * (1 + blocks),
        scratch_shapes=[
            pltpu.SMEM(lengths.shape, lengths.dtype),
            pltpu.SemaphoreType.DMA,
            pltpu.VMEM((heads // 2, tokens, 2 * group, width), BF16),
            pltpu.SemaphoreType.DMA((heads // 2,)),
        ],
        compiler_params=pltpu.CompilerParams(vmem_limit_bytes=24 * 2**20),
        name="prepare",
    )(*(pltpu.with_memory_space_constraint(x, HBM) for x in (lengths, queries)))
    return qh, masks


def early(qh, masks, mine, sibling):
    heads, rows, width = qh.shape
    count, tokens = len(mine), masks[0].shape[0] // 2
    group = rows // tokens
    shape = jax.ShapeDtypeStruct
    return pl.pallas_call(
        functools.partial(early_kernel, count, heads, group),
        out_shape=[shape((heads, width, rows), F32), shape((heads, rows), F32), shape((heads, rows), F32)],
        in_specs=[WHOLE] * (1 + 3 * count),
        out_specs=[WHOLE] * 3,
        compiler_params=pltpu.CompilerParams(vmem_limit_bytes=24 * 2**20),
        cost_estimate=cost(tokens, heads * group, width, count),
        name="early",
    )(qh, *masks, *mine, *sibling)


def middle(state, qh, mask, both):
    heads, rows, width = qh.shape
    tokens = mask.shape[0] // 2
    group = rows // tokens
    return pl.pallas_call(
        functools.partial(middle_kernel, heads, group),
        out_shape=[jax.ShapeDtypeStruct(x.shape, x.dtype) for x in state],
        in_specs=[WHOLE] * 6,
        out_specs=[WHOLE] * 3,
        compiler_params=pltpu.CompilerParams(vmem_limit_bytes=24 * 2**20),
        cost_estimate=cost(tokens, heads * group, width, 1),
        name="middle",
    )(qh, mask, *state, both)


def last(state, qh, masks, mine, sibling):
    heads, rows, width = qh.shape
    count, tokens = len(mine), masks[0].shape[0] // 2
    group = rows // tokens
    return pl.pallas_call(
        functools.partial(last_kernel, count, heads, group),
        out_shape=jax.ShapeDtypeStruct((tokens, heads * group, width), BF16),
        in_specs=[WHOLE] * (4 + 3 * count),
        out_specs=pl.BlockSpec(memory_space=HBM),
        scratch_shapes=[
            pltpu.VMEM((heads // 2, tokens, 2 * group, width), BF16),
            pltpu.SemaphoreType.DMA((heads // 2,)),
        ],
        compiler_params=pltpu.CompilerParams(vmem_limit_bytes=24 * 2**20),
        cost_estimate=cost(tokens, heads * group, width, count),
        name="last",
    )(qh, *state, *masks, *mine, *sibling)


def shards(queries, keys, values, key_scales, value_scales, lengths):
    tokens, heads, _ = keys.shape
    ranks = lax.axis_size("ctx")
    c = lax.axis_index("ctx")
    own = pack(keys, values, key_scales, value_scales)

    def send(value, target):
        pairs = [(source, target(source)) for source in range(ranks)]
        return lax.ppermute(value, "ctx", [(i, j) for i, j in pairs if 0 <= j < ranks])

    def swap(value):
        return lax.ppermute(value, "tp", [(0, 1), (1, 0)])

    k = c % 4
    even = k % 2 == 0
    from_z = send(own, lambda i: (i + 4) % ranks)
    from_d = send(own, lambda i: i + (3 if i % 2 == 0 else 1))
    qh, masks = prepare(queries, lengths, heads)
    from_z, masks[0] = lax.optimization_barrier((from_z, masks[0]))
    from_x = send(jnp.where(even, own, from_z), lambda i: i ^ 1)
    from_y = send(jnp.where(k < 2, own, from_z), lambda i: i ^ 2)
    acc, top, total = early(qh, masks[:2], [own, from_z], [swap(own), swap(from_z)])
    from_d, top = lax.optimization_barrier((from_d, top))
    both_d = lax.all_gather(from_d, "tp", axis=0, tiled=True)
    acc, top, total = middle((acc, top, total), qh, masks[GATHERED], both_d)
    from_x, top = lax.optimization_barrier((from_x, top))
    from_y, top = lax.optimization_barrier((from_y, top))
    size = from_x.shape[0]
    beside_x = swap(jnp.concatenate([from_x, masks[3]], axis=0))[:size]
    return last((acc, top, total), qh, masks[3:], [from_x, from_y], [beside_x, swap(from_y)])


def solution(mesh):
    both = P(("ctx", "tp"), None, None)
    return jax.shard_map(
        shards,
        mesh=mesh,
        in_specs=(both, both, both, P("ctx", "tp"), P("ctx", "tp"), P()),
        out_specs=both,
        check_vma=False,
    )
```

```python
import functools
import math

import jax
import jax.numpy as jnp
from jax import lax
from jax.experimental import pallas as pl
from jax.experimental.pallas import tpu as pltpu
from jax.sharding import PartitionSpec as P

NEG = -1e30
VMEM = pltpu.MemorySpace.VMEM
HBM = pltpu.MemorySpace.HBM
F32 = jnp.float32
BF16 = jnp.bfloat16
WHOLE = pl.BlockSpec(memory_space=VMEM)
SCALE_ROWS = 16
CHUNK = 256
GATHERED = 2


def pack_kernel(k_ref, v_ref, ks_ref, vs_ref, out_ref, rows_ref):
    tokens, heads, width = k_ref.shape
    for part, ref in enumerate((k_ref, v_ref)):
        rows_ref[part] = ref[...].astype(F32).reshape(tokens * heads, width)
        for head in range(heads):
            start = (part * heads + head) * tokens
            rows = rows_ref[part, pl.ds(head, tokens, stride=heads), :]
            out_ref[start : start + tokens, :] = rows.astype(out_ref.dtype)
    held = ks_ref.shape[1]
    row = lax.broadcasted_iota(jnp.int32, (SCALE_ROWS, held), 0)
    col = lax.broadcasted_iota(jnp.int32, (SCALE_ROWS, held), 1)
    k_scale = jnp.broadcast_to(ks_ref[...].astype(F32), row.shape)
    v_scale = jnp.broadcast_to(vs_ref[...].astype(F32), row.shape)
    both = jnp.where(row == col, k_scale, 0.0) + jnp.where(row == col + held, v_scale, 0.0)
    both = jnp.broadcast_to(jnp.sum(both, axis=1, keepdims=True), (SCALE_ROWS, width))
    out_ref[2 * heads * tokens :, :] = both.astype(out_ref.dtype)


def pack(keys, values, key_scales, value_scales):
    tokens, heads, width = keys.shape
    args = [pltpu.with_memory_space_constraint(x, HBM) for x in (keys, values, key_scales, value_scales)]
    return pl.pallas_call(
        pack_kernel,
        out_shape=jax.ShapeDtypeStruct((2 * heads * tokens + SCALE_ROWS, width), keys.dtype),
        grid=(1,),
        in_specs=[pl.BlockSpec(x.shape, lambda i, n=x.ndim: (0,) * n) for x in (keys, values, key_scales, value_scales)],
        out_specs=WHOLE,
        scratch_shapes=[pltpu.VMEM((2, tokens * heads, width), F32)],
        compiler_params=pltpu.CompilerParams(vmem_limit_bytes=8 * 2**20),
        name="pack",
    )(*args)


def scales_of(mine, sibling, heads, tokens, first):
    low = 2 * heads * tokens
    out = []
    for m, s in zip(mine, sibling):
        a, z = m[low:, :].astype(F32), s[low:, :].astype(F32)
        a, z = jnp.where(a > 0, a, 1.0), jnp.where(z > 0, z, 1.0)
        out.append((jnp.where(first, a, z), jnp.where(first, z, a)))
    return out


def attend_blocks(get_q, put, mask, mine, sibling, scale, heads, tokens, group, width, old):
    count = len(mine)
    block = 2 * tokens
    rows = tokens * group
    local = heads // 2
    chunk = min(CHUNK, rows)
    row_token = lax.broadcasted_iota(jnp.int32, (rows, width), 0) // group
    one_hot = jnp.where(row_token == lax.broadcasted_iota(jnp.int32, (rows, width), 1), 1.0, 0.0).astype(BF16)
    of_key = lax.broadcasted_iota(jnp.int32, (block * count, width), 0) // block
    ones = jnp.where(of_key == lax.broadcasted_iota(jnp.int32, (block * count, width), 1), 1.0, 0.0).astype(BF16)
    units = [(h, slice(r, r + chunk)) for h in range(heads) for r in range(0, rows, chunk)]
    ready = {}

    def stacked(at):
        return jnp.concatenate([r[at : at + tokens, :] for b in range(count) for r in (mine[b], sibling[b])], axis=0)

    def wide(x):
        return jnp.concatenate([x] * (chunk // width), axis=1)

    def prepared(h):
        if h not in ready:
            keys = jnp.concatenate([stacked(h * tokens), mask], axis=1)
            q = jnp.concatenate([get_q(h), one_hot], axis=1)
            part, at = h // local, h % local
            ks = [wide(s[part][at : at + 1, :] * (math.log2(math.e) / math.sqrt(width))) for s in scale]
            vs = [wide(s[part][local + at : local + at + 1, :]) for s in scale]
            ready[h] = keys, q, ks, [jnp.log2(v) for v in vs], [1.0 / v for v in vs]
        return ready[h]

    def scores_of(h, cs):
        keys, q = prepared(h)[:2]
        return lax.dot_general(keys, q[cs], (((1,), (1,)), ((), ())), preferred_element_type=F32)

    def softmax(h, cs, scores):
        ks, lv = prepared(h)[2:4]
        parts = [scores[b * block : (b + 1) * block] * ks[b] for b in range(count)]
        top = functools.reduce(jnp.maximum, [jnp.max(p, axis=0, keepdims=True) for p in parts])
        factor = None
        if old is not None:
            before = old[0][h : h + 1, cs]
            top = jnp.maximum(top, before)
            factor = jnp.exp2(before - top)
        weights = [jnp.exp2(parts[b] - (top - lv[b])).astype(BF16) for b in range(count)]
        return jnp.concatenate(weights, axis=0), top, factor

    def finish(h, cs, weights, top, factor):
        iv = prepared(h)[4]
        values = jnp.concatenate([stacked((heads + h) * tokens), ones], axis=1)
        acc = lax.dot_general(values, weights, (((0,), (0,)), ((), ())), preferred_element_type=F32)
        total = functools.reduce(jnp.add, [acc[width + b : width + b + 1] * iv[b] for b in range(count)])
        acc = acc[:width]
        if factor is not None:
            total = total + old[1][h : h + 1, cs] * factor
            acc = acc + old[2][h, :, cs] * factor
        put(h, cs, acc, top, total)

    scores = scores_of(*units[0])
    waiting = None
    for i, (h, cs) in enumerate(units):
        following = scores_of(*units[i + 1]) if i + 1 < len(units) else None
        done = softmax(h, cs, scores)
        if waiting is not None:
            finish(*waiting)
        waiting = (h, cs) + done
        scores = following
    finish(*waiting)


def prepare_kernel(heads, group, length_hbm, q_ref, qh_ref, *refs):
    masks, (length_ref, length_sem, q_buf, q_sem) = refs[:-4], refs[-4:]
    tokens, _, width = q_ref.shape
    rows, block, pair = tokens * group, 2 * tokens, 2 * group
    copies = [
        pltpu.make_async_copy(q_ref.at[:, pl.ds(g * pair, pair), :], q_buf.at[g], q_sem.at[g]) for g in range(heads // 2)
    ]
    lengths = pltpu.make_async_copy(length_hbm, length_ref, length_sem)
    lengths.start()
    for copy in copies:
        copy.start()
    chip, core = lax.axis_index("ctx"), lax.axis_index("tp")
    even = chip % 2 == 0
    position = chip * block + core * tokens + lax.broadcasted_iota(jnp.int32, (8, width), 1)

    def later(i, carry):
        start, end = carry
        end = end + length_ref[i]
        return jnp.where(position >= end, end, start), end

    lengths.wait()
    start, _ = lax.fori_loop(0, length_ref.shape[0], later, (jnp.zeros_like(position), jnp.int32(0)))
    start, position = start[:1], position[:1]
    i = lax.broadcasted_iota(jnp.int32, (block, width), 0)
    offset = jnp.where(i < tokens, core * tokens + i, (1 - core) * tokens + i - tokens)
    for b, back in enumerate((0, 4, jnp.where(even, 1, 3), jnp.where(even, 3, 1), 2)):
        key = (chip - back) * block + (i if b == GATHERED else offset)
        masks[b][...] = jnp.where((key >= start) & (key <= position), 0.0, NEG).astype(BF16)
    for h in range(heads):
        if h % 2 == 0:
            copies[h // 2].wait()
        qh_ref[h] = q_buf[h // 2][:, (h % 2) * group : (h % 2 + 1) * group, :].reshape(rows, width)


def early_kernel(count, heads, group, qh_ref, *refs):
    masks, mine, sibling = refs[:count], refs[count : 2 * count], refs[2 * count : 3 * count]
    acc_ref, top_ref, sum_ref = refs[3 * count :]
    _, rows, width = qh_ref.shape
    tokens = rows // group
    scale = scales_of(mine, sibling, heads, tokens, lax.axis_index("tp") == 0)
    mask = jnp.concatenate([ref[...] for ref in masks], axis=0)

    def put(h, cs, acc, top, total):
        acc_ref[h, :, cs] = acc
        top_ref[h : h + 1, cs] = top
        sum_ref[h : h + 1, cs] = total

    attend_blocks(lambda h: qh_ref[h], put, mask, mine, sibling, scale, heads, tokens, group, width, None)


def middle_kernel(heads, group, qh_ref, mask_ref, acc_ref, top_ref, sum_ref, both_ref, acc_out, top_out, sum_out):
    _, rows, width = qh_ref.shape
    tokens = rows // group
    size = both_ref.shape[0] // 2
    mine, sibling = [both_ref.at[:size]], [both_ref.at[size:]]
    scale = scales_of(mine, sibling, heads, tokens, True)

    def put(h, cs, acc, top, total):
        acc_out[h, :, cs] = acc
        top_out[h : h + 1, cs] = top
        sum_out[h : h + 1, cs] = total

    attend_blocks(
        lambda h: qh_ref[h], put, mask_ref[...], mine, sibling, scale, heads, tokens, group, width, (top_ref, sum_ref, acc_ref)
    )


def last_kernel(count, heads, group, qh_ref, acc_ref, top_ref, sum_ref, *refs):
    masks, mine, sibling = refs[:count], refs[count : 2 * count], refs[2 * count : 3 * count]
    out_ref, o_buf, o_sem = refs[3 * count :]
    _, rows, width = qh_ref.shape
    tokens, pair = rows // group, 2 * group
    scale = scales_of(mine, sibling, heads, tokens, lax.axis_index("tp") == 0)
    mask = jnp.concatenate([ref[...] for ref in masks], axis=0)
    copies = []

    def put(h, cs, acc, top, total):
        out = (acc * (1.0 / total)).astype(BF16).T
        span = slice(cs.start // group, cs.stop // group)
        o_buf[h // 2, span, (h % 2) * group : (h % 2 + 1) * group, :] = out.reshape(span.stop - span.start, group, width)
        if h % 2 == 1 and cs.stop == rows:
            g = h // 2
            copies.append(pltpu.make_async_copy(o_buf.at[g], out_ref.at[:, pl.ds(g * pair, pair), :], o_sem.at[g]))
            copies[-1].start()

    attend_blocks(
        lambda h: qh_ref[h], put, mask, mine, sibling, scale, heads, tokens, group, width, (top_ref, sum_ref, acc_ref)
    )
    for copy in copies:
        copy.wait()


def cost(tokens, q_heads, width, blocks):
    work = tokens * q_heads * blocks * 2 * tokens
    return pl.CostEstimate(flops=4 * work * width, bytes_accessed=2 * tokens * q_heads * width, transcendentals=work)


def prepare(queries, lengths, heads, blocks=5):
    tokens, q_heads, width = queries.shape
    group = q_heads // heads
    out = [((heads, tokens * group, width), BF16)] + [((2 * tokens, width), BF16)] * blocks
    qh, *masks = pl.pallas_call(
        functools.partial(prepare_kernel, heads, group),
        out_shape=[jax.ShapeDtypeStruct(*x) for x in out],
        in_specs=[pl.BlockSpec(memory_space=HBM)] * 2,
        out_specs=[WHOLE] * (1 + blocks),
        scratch_shapes=[
            pltpu.SMEM(lengths.shape, lengths.dtype),
            pltpu.SemaphoreType.DMA,
            pltpu.VMEM((heads // 2, tokens, 2 * group, width), BF16),
            pltpu.SemaphoreType.DMA((heads // 2,)),
        ],
        compiler_params=pltpu.CompilerParams(vmem_limit_bytes=24 * 2**20),
        name="prepare",
    )(*(pltpu.with_memory_space_constraint(x, HBM) for x in (lengths, queries)))
    return qh, masks


def early(qh, masks, mine, sibling):
    heads, rows, width = qh.shape
    count, tokens = len(mine), masks[0].shape[0] // 2
    group = rows // tokens
    shape = jax.ShapeDtypeStruct
    return pl.pallas_call(
        functools.partial(early_kernel, count, heads, group),
        out_shape=[shape((heads, width, rows), F32), shape((heads, rows), F32), shape((heads, rows), F32)],
        in_specs=[WHOLE] * (1 + 3 * count),
        out_specs=[WHOLE] * 3,
        compiler_params=pltpu.CompilerParams(vmem_limit_bytes=24 * 2**20),
        cost_estimate=cost(tokens, heads * group, width, count),
        name="early",
    )(qh, *masks, *mine, *sibling)


def middle(state, qh, mask, both):
    heads, rows, width = qh.shape
    tokens = mask.shape[0] // 2
    group = rows // tokens
    return pl.pallas_call(
        functools.partial(middle_kernel, heads, group),
        out_shape=[jax.ShapeDtypeStruct(x.shape, x.dtype) for x in state],
        in_specs=[WHOLE] * 6,
        out_specs=[WHOLE] * 3,
        compiler_params=pltpu.CompilerParams(vmem_limit_bytes=24 * 2**20),
        cost_estimate=cost(tokens, heads * group, width, 1),
        name="middle",
    )(qh, mask, *state, both)


def last(state, qh, masks, mine, sibling):
    heads, rows, width = qh.shape
    count, tokens = len(mine), masks[0].shape[0] // 2
    group = rows // tokens
    return pl.pallas_call(
        functools.partial(last_kernel, count, heads, group),
        out_shape=jax.ShapeDtypeStruct((tokens, heads * group, width), BF16),
        in_specs=[WHOLE] * (4 + 3 * count),
        out_specs=pl.BlockSpec(memory_space=HBM),
        scratch_shapes=[
            pltpu.VMEM((heads // 2, tokens, 2 * group, width), BF16),
            pltpu.SemaphoreType.DMA((heads // 2,)),
        ],
        compiler_params=pltpu.CompilerParams(vmem_limit_bytes=24 * 2**20),
        cost_estimate=cost(tokens, heads * group, width, count),
        name="last",
    )(qh, *state, *masks, *mine, *sibling)


def shards(queries, keys, values, key_scales, value_scales, lengths):
    tokens, heads, _ = keys.shape
    ranks = lax.axis_size("ctx")
    c = lax.axis_index("ctx")
    own = pack(keys, values, key_scales, value_scales)

    def send(value, target):
        pairs = [(source, target(source)) for source in range(ranks)]
        return lax.ppermute(value, "ctx", [(i, j) for i, j in pairs if 0 <= j < ranks])

    def swap(value):
        return lax.ppermute(value, "tp", [(0, 1), (1, 0)])

    k = c % 4
    even = k % 2 == 0
    from_z = send(own, lambda i: (i + 4) % ranks)
    from_d = send(own, lambda i: i + (3 if i % 2 == 0 else 1))
    qh, masks = prepare(queries, lengths, heads)
    from_z, masks[0] = lax.optimization_barrier((from_z, masks[0]))
    from_x = send(jnp.where(even, own, from_z), lambda i: i ^ 1)
    from_y = send(jnp.where(k < 2, own, from_z), lambda i: i ^ 2)
    acc, top, total = early(qh, masks[:2], [own, from_z], [swap(own), swap(from_z)])
    from_d, top = lax.optimization_barrier((from_d, top))
    both_d = lax.all_gather(from_d, "tp", axis=0, tiled=True)
    acc, top, total = middle((acc, top, total), qh, masks[GATHERED], both_d)
    from_x, top = lax.optimization_barrier((from_x, top))
    from_y, top = lax.optimization_barrier((from_y, top))
    size = from_x.shape[0]
    beside_x = swap(jnp.concatenate([from_x, masks[3][:SCALE_ROWS]], axis=0))[:size]
    return last((acc, top, total), qh, masks[3:], [from_x, from_y], [beside_x, swap(from_y)])


def solution(mesh):
    both = P(("ctx", "tp"), None, None)
    return jax.shard_map(
        shards,
        mesh=mesh,
        in_specs=(both, both, both, P("ctx", "tp"), P("ctx", "tp"), P()),
        out_specs=both,
        check_vma=False,
    )
```

```python
import functools
import math

import jax
import jax.numpy as jnp
from jax import lax
from jax.experimental import pallas as pl
from jax.experimental.pallas import tpu as pltpu
from jax.sharding import PartitionSpec as P

NEG = -1e30
VMEM = pltpu.MemorySpace.VMEM
HBM = pltpu.MemorySpace.HBM
F32 = jnp.float32
BF16 = jnp.bfloat16
WHOLE = pl.BlockSpec(memory_space=VMEM)
SCALE_ROWS = 16
CHUNK = 256
GATHERED = 2


def pack_kernel(k_ref, v_ref, ks_ref, vs_ref, out_ref, rows_ref):
    tokens, heads, width = k_ref.shape
    for part, ref in enumerate((k_ref, v_ref)):
        rows_ref[part] = ref[...].astype(F32).reshape(tokens * heads, width)
        for head in range(heads):
            start = (part * heads + head) * tokens
            rows = rows_ref[part, pl.ds(head, tokens, stride=heads), :]
            out_ref[start : start + tokens, :] = rows.astype(out_ref.dtype)
    held = ks_ref.shape[1]
    row = lax.broadcasted_iota(jnp.int32, (SCALE_ROWS, held), 0)
    col = lax.broadcasted_iota(jnp.int32, (SCALE_ROWS, held), 1)
    k_scale = jnp.broadcast_to(ks_ref[...].astype(F32), row.shape)
    v_scale = jnp.broadcast_to(vs_ref[...].astype(F32), row.shape)
    both = jnp.where(row == col, k_scale, 0.0) + jnp.where(row == col + held, v_scale, 0.0)
    both = jnp.broadcast_to(jnp.sum(both, axis=1, keepdims=True), (SCALE_ROWS, width))
    out_ref[2 * heads * tokens :, :] = both.astype(out_ref.dtype)


def pack(keys, values, key_scales, value_scales):
    tokens, heads, width = keys.shape
    args = [pltpu.with_memory_space_constraint(x, HBM) for x in (keys, values, key_scales, value_scales)]
    return pl.pallas_call(
        pack_kernel,
        out_shape=jax.ShapeDtypeStruct((2 * heads * tokens + SCALE_ROWS, width), keys.dtype),
        grid=(1,),
        in_specs=[pl.BlockSpec(x.shape, lambda i, n=x.ndim: (0,) * n) for x in (keys, values, key_scales, value_scales)],
        out_specs=WHOLE,
        scratch_shapes=[pltpu.VMEM((2, tokens * heads, width), F32)],
        compiler_params=pltpu.CompilerParams(vmem_limit_bytes=8 * 2**20),
        name="pack",
    )(*args)


def scales_of(mine, sibling, heads, tokens, first):
    low = 2 * heads * tokens
    out = []
    for m, s in zip(mine, sibling):
        a, z = m[low:, :].astype(F32), s[low:, :].astype(F32)
        a, z = jnp.where(a > 0, a, 1.0), jnp.where(z > 0, z, 1.0)
        out.append((jnp.where(first, a, z), jnp.where(first, z, a)))
    return out


def attend_blocks(get_q, put, mask, mine, sibling, scale, heads, tokens, group, width, old):
    count = len(mine)
    block = 2 * tokens
    rows = tokens * group
    local = heads // 2
    chunk = min(CHUNK, rows)
    row_token = lax.broadcasted_iota(jnp.int32, (rows, width), 0) // group
    one_hot = jnp.where(row_token == lax.broadcasted_iota(jnp.int32, (rows, width), 1), 1.0, 0.0).astype(BF16)
    of_key = lax.broadcasted_iota(jnp.int32, (block * count, width), 0) // block
    ones = jnp.where(of_key == lax.broadcasted_iota(jnp.int32, (block * count, width), 1), 1.0, 0.0).astype(BF16)
    units = [(h, slice(r, r + chunk)) for h in range(heads) for r in range(0, rows, chunk)]
    ready = {}

    def stacked(at):
        return jnp.concatenate([r[at : at + tokens, :] for b in range(count) for r in (mine[b], sibling[b])], axis=0)

    def wide(x):
        return jnp.concatenate([x] * (chunk // width), axis=1)

    def prepared(h):
        if h not in ready:
            keys = jnp.concatenate([stacked(h * tokens), mask], axis=1)
            q = jnp.concatenate([get_q(h), one_hot], axis=1)
            part, at = h // local, h % local
            ks = [wide(s[part][at : at + 1, :] * (math.log2(math.e) / math.sqrt(width))) for s in scale]
            vs = [wide(s[part][local + at : local + at + 1, :]) for s in scale]
            ready[h] = keys, q, ks, [jnp.log2(v) for v in vs], [1.0 / v for v in vs]
        return ready[h]

    def scores_of(h, cs):
        keys, q = prepared(h)[:2]
        return lax.dot_general(keys, q[cs], (((1,), (1,)), ((), ())), preferred_element_type=F32)

    def softmax(h, cs, scores):
        ks, lv = prepared(h)[2:4]
        parts = [scores[b * block : (b + 1) * block] * ks[b] for b in range(count)]
        top = functools.reduce(jnp.maximum, [jnp.max(p, axis=0, keepdims=True) for p in parts])
        factor = None
        if old is not None:
            before = old[0][h : h + 1, cs]
            top = jnp.maximum(top, before)
            factor = jnp.exp2(before - top)
        weights = [jnp.exp2(parts[b] - (top - lv[b])).astype(BF16) for b in range(count)]
        return jnp.concatenate(weights, axis=0), top, factor

    def finish(h, cs, weights, top, factor):
        iv = prepared(h)[4]
        values = jnp.concatenate([stacked((heads + h) * tokens), ones], axis=1)
        acc = lax.dot_general(values, weights, (((0,), (0,)), ((), ())), preferred_element_type=F32)
        total = functools.reduce(jnp.add, [acc[width + b : width + b + 1] * iv[b] for b in range(count)])
        acc = acc[:width]
        if factor is not None:
            total = total + old[1][h : h + 1, cs] * factor
            acc = acc + old[2][h, :, cs] * factor
        put(h, cs, acc, top, total)

    scores = scores_of(*units[0])
    waiting = None
    for i, (h, cs) in enumerate(units):
        following = scores_of(*units[i + 1]) if i + 1 < len(units) else None
        done = softmax(h, cs, scores)
        if waiting is not None:
            finish(*waiting)
        waiting = (h, cs) + done
        scores = following
    finish(*waiting)


def prepare_kernel(heads, group, length_hbm, q_ref, qh_ref, *refs):
    masks, (length_ref, length_sem, q_buf, q_sem) = refs[:-4], refs[-4:]
    tokens, _, width = q_ref.shape
    rows, block, pair = tokens * group, 2 * tokens, 2 * group
    copies = [
        pltpu.make_async_copy(q_ref.at[:, pl.ds(g * pair, pair), :], q_buf.at[g], q_sem.at[g]) for g in range(heads // 2)
    ]
    lengths = pltpu.make_async_copy(length_hbm, length_ref, length_sem)
    lengths.start()
    for copy in copies:
        copy.start()
    chip, core = lax.axis_index("ctx"), lax.axis_index("tp")
    even = chip % 2 == 0
    position = chip * block + core * tokens + lax.broadcasted_iota(jnp.int32, (8, width), 1)

    def later(i, carry):
        start, end = carry
        end = end + length_ref[i]
        return jnp.where(position >= end, end, start), end

    lengths.wait()
    start, _ = lax.fori_loop(0, length_ref.shape[0], later, (jnp.zeros_like(position), jnp.int32(0)))
    start, position = start[:1], position[:1]
    i = lax.broadcasted_iota(jnp.int32, (block, width), 0)
    offset = jnp.where(i < tokens, core * tokens + i, (1 - core) * tokens + i - tokens)
    for b, back in enumerate((0, 4, jnp.where(even, 1, 3), jnp.where(even, 3, 1), 2)):
        key = (chip - back) * block + (i if b == GATHERED else offset)
        masks[b][...] = jnp.where((key >= start) & (key <= position), 0.0, NEG).astype(BF16)
    for h in range(heads):
        if h % 2 == 0:
            copies[h // 2].wait()
        qh_ref[h] = q_buf[h // 2][:, (h % 2) * group : (h % 2 + 1) * group, :].reshape(rows, width)


def early_kernel(count, heads, group, qh_ref, *refs):
    masks, mine, sibling = refs[:count], refs[count : 2 * count], refs[2 * count : 3 * count]
    acc_ref, top_ref, sum_ref = refs[3 * count :]
    _, rows, width = qh_ref.shape
    tokens = rows // group
    scale = scales_of(mine, sibling, heads, tokens, lax.axis_index("tp") == 0)
    mask = jnp.concatenate([ref[...] for ref in masks], axis=0)

    def put(h, cs, acc, top, total):
        acc_ref[h, :, cs] = acc
        top_ref[h : h + 1, cs] = top
        sum_ref[h : h + 1, cs] = total

    attend_blocks(lambda h: qh_ref[h], put, mask, mine, sibling, scale, heads, tokens, group, width, None)


def middle_kernel(heads, group, qh_ref, mask_ref, acc_ref, top_ref, sum_ref, both_ref, acc_out, top_out, sum_out):
    _, rows, width = qh_ref.shape
    tokens = rows // group
    size = both_ref.shape[0] // 2
    mine, sibling = [both_ref.at[:size]], [both_ref.at[size:]]
    scale = scales_of(mine, sibling, heads, tokens, True)

    def put(h, cs, acc, top, total):
        acc_out[h, :, cs] = acc
        top_out[h : h + 1, cs] = top
        sum_out[h : h + 1, cs] = total

    attend_blocks(
        lambda h: qh_ref[h], put, mask_ref[...], mine, sibling, scale, heads, tokens, group, width, (top_ref, sum_ref, acc_ref)
    )


def last_kernel(count, heads, group, qh_ref, acc_ref, top_ref, sum_ref, *refs):
    masks, mine, sibling = refs[:count], refs[count : 2 * count], refs[2 * count : 3 * count]
    out_ref, o_buf, o_sem = refs[3 * count :]
    _, rows, width = qh_ref.shape
    tokens, pair = rows // group, 2 * group
    scale = scales_of(mine, sibling, heads, tokens, lax.axis_index("tp") == 0)
    mask = jnp.concatenate([ref[...] for ref in masks], axis=0)
    copies = []

    def put(h, cs, acc, top, total):
        out = (acc * (1.0 / total)).astype(BF16).T
        span = slice(cs.start // group, cs.stop // group)
        o_buf[h // 2, span, (h % 2) * group : (h % 2 + 1) * group, :] = out.reshape(span.stop - span.start, group, width)
        if h % 2 == 1:
            g, at = h // 2, pl.ds(span.start, span.stop - span.start)
            target = out_ref.at[at, pl.ds(g * pair, pair), :]
            copies.append(pltpu.make_async_copy(o_buf.at[g, at], target, o_sem.at[len(copies)]))
            copies[-1].start()

    attend_blocks(
        lambda h: qh_ref[h], put, mask, mine, sibling, scale, heads, tokens, group, width, (top_ref, sum_ref, acc_ref)
    )
    for copy in copies:
        copy.wait()


def cost(tokens, q_heads, width, blocks):
    work = tokens * q_heads * blocks * 2 * tokens
    return pl.CostEstimate(flops=4 * work * width, bytes_accessed=2 * tokens * q_heads * width, transcendentals=work)


def prepare(queries, lengths, heads, blocks=5):
    tokens, q_heads, width = queries.shape
    group = q_heads // heads
    out = [((heads, tokens * group, width), BF16)] + [((2 * tokens, width), BF16)] * blocks
    qh, *masks = pl.pallas_call(
        functools.partial(prepare_kernel, heads, group),
        out_shape=[jax.ShapeDtypeStruct(*x) for x in out],
        in_specs=[pl.BlockSpec(memory_space=HBM)] * 2,
        out_specs=[WHOLE] * (1 + blocks),
        scratch_shapes=[
            pltpu.SMEM(lengths.shape, lengths.dtype),
            pltpu.SemaphoreType.DMA,
            pltpu.VMEM((heads // 2, tokens, 2 * group, width), BF16),
            pltpu.SemaphoreType.DMA((heads // 2,)),
        ],
        compiler_params=pltpu.CompilerParams(vmem_limit_bytes=24 * 2**20),
        name="prepare",
    )(*(pltpu.with_memory_space_constraint(x, HBM) for x in (lengths, queries)))
    return qh, masks


def early(qh, masks, mine, sibling):
    heads, rows, width = qh.shape
    count, tokens = len(mine), masks[0].shape[0] // 2
    group = rows // tokens
    shape = jax.ShapeDtypeStruct
    return pl.pallas_call(
        functools.partial(early_kernel, count, heads, group),
        out_shape=[shape((heads, width, rows), F32), shape((heads, rows), F32), shape((heads, rows), F32)],
        in_specs=[WHOLE] * (1 + 3 * count),
        out_specs=[WHOLE] * 3,
        compiler_params=pltpu.CompilerParams(vmem_limit_bytes=24 * 2**20),
        cost_estimate=cost(tokens, heads * group, width, count),
        name="early",
    )(qh, *masks, *mine, *sibling)


def middle(state, qh, mask, both):
    heads, rows, width = qh.shape
    tokens = mask.shape[0] // 2
    group = rows // tokens
    return pl.pallas_call(
        functools.partial(middle_kernel, heads, group),
        out_shape=[jax.ShapeDtypeStruct(x.shape, x.dtype) for x in state],
        in_specs=[WHOLE] * 6,
        out_specs=[WHOLE] * 3,
        compiler_params=pltpu.CompilerParams(vmem_limit_bytes=24 * 2**20),
        cost_estimate=cost(tokens, heads * group, width, 1),
        name="middle",
    )(qh, mask, *state, both)


def last(state, qh, masks, mine, sibling):
    heads, rows, width = qh.shape
    count, tokens = len(mine), masks[0].shape[0] // 2
    group = rows // tokens
    return pl.pallas_call(
        functools.partial(last_kernel, count, heads, group),
        out_shape=jax.ShapeDtypeStruct((tokens, heads * group, width), BF16),
        in_specs=[WHOLE] * (4 + 3 * count),
        out_specs=pl.BlockSpec(memory_space=HBM),
        scratch_shapes=[
            pltpu.VMEM((heads // 2, tokens, 2 * group, width), BF16),
            pltpu.SemaphoreType.DMA((heads // 2 * (rows // min(CHUNK, rows)),)),
        ],
        compiler_params=pltpu.CompilerParams(vmem_limit_bytes=24 * 2**20),
        cost_estimate=cost(tokens, heads * group, width, count),
        name="last",
    )(qh, *state, *masks, *mine, *sibling)


def shards(queries, keys, values, key_scales, value_scales, lengths):
    tokens, heads, _ = keys.shape
    ranks = lax.axis_size("ctx")
    c = lax.axis_index("ctx")
    own = pack(keys, values, key_scales, value_scales)

    def send(value, target):
        pairs = [(source, target(source)) for source in range(ranks)]
        return lax.ppermute(value, "ctx", [(i, j) for i, j in pairs if 0 <= j < ranks])

    def swap(value):
        return lax.ppermute(value, "tp", [(0, 1), (1, 0)])

    k = c % 4
    even = k % 2 == 0
    from_z = send(own, lambda i: (i + 4) % ranks)
    from_d = send(own, lambda i: i + (3 if i % 2 == 0 else 1))
    qh, masks = prepare(queries, lengths, heads)
    from_z, masks[0] = lax.optimization_barrier((from_z, masks[0]))
    from_x = send(jnp.where(even, own, from_z), lambda i: i ^ 1)
    from_y = send(jnp.where(k < 2, own, from_z), lambda i: i ^ 2)
    acc, top, total = early(qh, masks[:2], [own, from_z], [swap(own), swap(from_z)])
    from_d, top = lax.optimization_barrier((from_d, top))
    both_d = lax.all_gather(from_d, "tp", axis=0, tiled=True)
    acc, top, total = middle((acc, top, total), qh, masks[GATHERED], both_d)
    from_x, top = lax.optimization_barrier((from_x, top))
    from_y, top = lax.optimization_barrier((from_y, top))
    size = from_x.shape[0]
    beside_x = swap(jnp.concatenate([from_x, masks[3][:SCALE_ROWS]], axis=0))[:size]
    return last((acc, top, total), qh, masks[3:], [from_x, from_y], [beside_x, swap(from_y)])


def solution(mesh):
    both = P(("ctx", "tp"), None, None)
    return jax.shard_map(
        shards,
        mesh=mesh,
        in_specs=(both, both, both, P("ctx", "tp"), P("ctx", "tp"), P()),
        out_specs=both,
        check_vma=False,
    )
```
